512 devices in a mesh: leaf: 128 (over y, z, core), coef: 4 (over x).
Axes of the slice: x: 4, y: 8, z: 8, core: 2. Of those that a mesh axis runs over, the one named last changes fastest.
Arguments:
- leaf_mult: bfloat16 [289, 524288], P(None, ('leaf', 'coef')), may hold values from -6 to 6
- fine_count: int32 [512], P(('leaf', 'coef')), may hold values from 256 to 1024, as said below
- parent_a: int32 [524288], P(('leaf', 'coef')), may hold values from 0 to 65535, as said below
- octant_a: int32 [524288], P(('leaf', 'coef')), may hold values from 0 to 7
- parent_b: int32 [65536], P(('leaf', 'coef')), may hold values from 0 to 8191, as said below
- octant_b: int32 [65536], P(('leaf', 'coef')), may hold values from 0 to 7
- parent_c: int32 [8192], P(('leaf', 'coef')), may hold values from 0 to 1023, as said below
- octant_c: int32 [8192], P(('leaf', 'coef')), may hold values from 0 to 7
- list_b_src: int32 [65536, 16], P(('leaf', 'coef')), may hold values from 0 to 65535, as said below
- list_b_off: int32 [65536, 16], P(('leaf', 'coef')), may hold values from 0 to 7
- list_t_src: int32 [1024, 16], replicated, may hold values from 0 to 1023
- list_t_off: int32 [1024, 16], replicated, may hold values from 0 to 7
- m2m_ops: bfloat16 [8, 289, 289], replicated, may hold values from -0.375 to 0.375
- m2l_ops: bfloat16 [8, 289, 289], replicated, may hold values from -0.375 to 0.375
Outputs:
- fine_local: bfloat16 [289, 524288], P(None, ('leaf', 'coef'))
The draws below stay inside these ranges and needn't reach their ends.
Inputs may be any that keep to these rules, and one draw needn't show every extreme that they name: `fine_count`: the living fine cells of a device are the first ones of its range; some device is full and some holds a quarter of 1024. `parent_a`: the parent of a fine cell is a level-B cell of the same device; parents never fall along the cells. `parent_b`: the parent of a level-B cell is a level-C cell of the same device; parents never fall along the cells. `parent_c`: parents never fall along the cells; the children of a top cell may lie on several devices. `list_b_src`: every source lies on the target's device or on the device just before or just after it in order.
All inputs are finite; a program needn't handle non-finite values.
Results may differ from the reference program's by a relative error of at most 0.02.
Values may be sent and summed in bfloat16 or wider, within the bound.
A program may use at most 64 MiB of HBM per device.

```python
import jax
import jax.numpy as jnp

K = 289
OFFSETS = 8
LB = 16
LT = 16
NA_DEV = 1024
NB_DEV = 128
NC_DEV = 16
NA = 524288
NB = 65536
NC = 8192
NT = 1024
DEVICES = 512


def rising(key, groups, per_group, targets):
    drawn = jnp.sort(jax.random.randint(key, (groups, per_group), 0, targets), axis=1)
    drawn = drawn.at[:, 0].set(0).at[:, per_group - 1].set(targets - 1)
    return (drawn + jnp.arange(groups, dtype=jnp.int32)[:, None] * targets).reshape(-1).astype(jnp.int32)


def draw_fine_count(key, part):
    key = jax.random.fold_in(key, 11)
    first, second, third = jax.random.split(key, 3)
    counts = jax.random.randint(first, (DEVICES,), NA_DEV // 4, NA_DEV + 1)
    full_device = jax.random.randint(second, (), 0, DEVICES)
    low_device = (full_device + 1 + jax.random.randint(third, (), 0, DEVICES - 1)) % DEVICES
    counts = counts.at[full_device].set(NA_DEV).at[low_device].set(NA_DEV // 4)
    return counts.astype(jnp.int32)


def draw_parent_a(key, part):
    key = jax.random.fold_in(key, 12)
    return rising(key, DEVICES, NA_DEV, NB_DEV)


def draw_parent_b(key, part):
    key = jax.random.fold_in(key, 13)
    return rising(key, DEVICES, NB_DEV, NC_DEV)


def draw_parent_c(key, part):
    key = jax.random.fold_in(key, 14)
    return rising(key, 1, NC, NT)


def draw_list_b_src(key, part):
    key = jax.random.fold_in(key, 15)
    owner = jnp.arange(NB, dtype=jnp.int32) // NB_DEV
    reach = jax.random.randint(key, (NB, LB), -NB_DEV, 2 * NB_DEV)
    return jnp.clip(owner[:, None] * NB_DEV + reach, 0, NB - 1).astype(jnp.int32)


def with_ends(result, rng, low, largest):
    extent = result.shape
    spot = [jax.random.randint(jax.random.fold_in(rng, axis), (), 0, extent[axis]) for axis in range(len(extent))]
    result = result.at[tuple(spot)].set(low)
    longest = extent.index(max(extent))
    spot[longest] = (spot[longest] + 1) % extent[longest]
    return result.at[tuple(spot)].set(largest)


def level_of(key, shape, shards, low, top_value):
    loudness, own = 1.0, jax.random.fold_in(key, 6)
    for dim, parts in shards:
        draws = jnp.exp(jax.random.uniform(jax.random.fold_in(own, dim), (parts,), jnp.float32, low / len(shards), top_value / len(shards)))
        loudness = loudness * jnp.repeat(draws, shape[dim] // parts).reshape([-1 if axis == dim else 1 for axis in range(len(shape))])
    return loudness


def gaussian(own_key, shape, deviation, bound, cuts=(), kind=jnp.bfloat16):
    array = deviation * jax.random.normal(own_key, shape, jnp.float32)
    if cuts:
        array = array * level_of(own_key, shape, cuts, -0.22, 0.18)
    return jnp.clip(array, -bound, bound).astype(kind)


def setup_inputs(seed: int = 0) -> dict:
    key_of = jax.random.split(jax.random.key(seed), 15)
    return {
        "leaf_mult": gaussian(key_of[0], (K, NA), 1.0, 6.0, ((1, 512),)),
        "fine_count": draw_fine_count(jax.random.fold_in(key_of[14], 71), 0),
        "parent_a": draw_parent_a(jax.random.fold_in(key_of[14], 71), 0),
        "octant_a": with_ends(jax.random.randint(key_of[3], (NA,), 0, 8), jax.random.fold_in(key_of[3], 1), 0, 7).astype(jnp.int32),
        "parent_b": draw_parent_b(jax.random.fold_in(key_of[14], 71), 0),
        "octant_b": with_ends(jax.random.randint(key_of[5], (NB,), 0, 8), jax.random.fold_in(key_of[5], 1), 0, 7).astype(jnp.int32),
        "parent_c": draw_parent_c(jax.random.fold_in(key_of[14], 71), 0),
        "octant_c": with_ends(jax.random.randint(key_of[7], (NC,), 0, 8), jax.random.fold_in(key_of[7], 1), 0, 7).astype(jnp.int32),
        "list_b_src": draw_list_b_src(jax.random.fold_in(key_of[14], 71), 0),
        "list_b_off": with_ends(jax.random.randint(key_of[9], (NB, LB), 0, OFFSETS), jax.random.fold_in(key_of[9], 1), 0, OFFSETS - 1).astype(jnp.int32),
        "list_t_src": with_ends(jax.random.randint(key_of[10], (NT, LT), 0, NT), jax.random.fold_in(key_of[10], 1), 0, NT - 1).astype(jnp.int32),
        "list_t_off": with_ends(jax.random.randint(key_of[11], (NT, LT), 0, OFFSETS), jax.random.fold_in(key_of[11], 1), 0, OFFSETS - 1).astype(jnp.int32),
        "m2m_ops": gaussian(key_of[12], (8, K, K), K ** -0.5, 0.375),
        "m2l_ops": gaussian(key_of[13], (OFFSETS, K, K), K ** -0.5, 0.375),
    }


def group_up(expansion, parent, octant, weight, segments):
    data = expansion.astype(jnp.float32).T * weight[:, None]
    summed = jax.ops.segment_sum(data, octant * segments + parent, num_segments=8 * segments)
    return summed.reshape(8, segments, K).transpose(0, 2, 1).astype(jnp.bfloat16)


def apply_stack(operators, stack):
    running = jnp.dot(operators[0], stack[0], preferred_element_type=jnp.float32)
    for which in range(1, operators.shape[0]):
        running = running + jnp.dot(operators[which], stack[which], preferred_element_type=jnp.float32)
    return running


def per_cell(operators, source, octant):
    running = jnp.zeros(source.shape, jnp.float32)
    for which in range(8):
        shifted = jnp.dot(operators[which], source, preferred_element_type=jnp.float32)
        running = running + jnp.where(octant[None, :] == which, shifted, 0.0)
    return running


def descend(operators, source, parent, octant):
    running = jnp.zeros((source.shape[0], parent.shape[0]), jnp.float32)
    for which in range(8):
        shifted = jnp.dot(operators[which].T, source, preferred_element_type=jnp.float32)
        running = running + jnp.where(octant[None, :] == which, jnp.take(shifted, parent, axis=1), 0.0)
    return running


def pack(source, sources, offsets, offset_kinds):
    targets, entries = sources.shape
    gathered = jnp.take(source, sources.reshape(-1), axis=1).reshape(source.shape[0], targets, entries)
    one_hot = (offsets[:, :, None] == jnp.arange(offset_kinds, dtype=jnp.int32)[None, None, :])
    packed = jnp.einsum("ktj,tjo->okt", gathered.astype(jnp.float32), one_hot.astype(jnp.float32))
    return packed.astype(jnp.bfloat16)


def reference(leaf_mult, fine_count, parent_a, octant_a, parent_b, octant_b, parent_c, octant_c, list_b_src, list_b_off, list_t_src, list_t_off, m2m_ops, m2l_ops):
    cell_index = jnp.arange(NA, dtype=jnp.int32)
    living = (cell_index % NA_DEV) < fine_count[cell_index // NA_DEV]
    grouped_b = group_up(leaf_mult, parent_a, octant_a, living.astype(jnp.float32), NB)
    mult_b = apply_stack(m2m_ops, grouped_b).astype(jnp.bfloat16)
    grouped_c = group_up(mult_b, parent_b, octant_b, jnp.ones((NB,), jnp.float32), NC)
    mult_c = apply_stack(m2m_ops, grouped_c).astype(jnp.bfloat16)
    shifted = per_cell(m2m_ops, mult_c, octant_c)
    top_mult = jax.ops.segment_sum(shifted.T, parent_c, num_segments=NT).T.astype(jnp.bfloat16)
    top_local = apply_stack(m2l_ops, pack(top_mult, list_t_src, list_t_off, OFFSETS)).astype(jnp.bfloat16)
    c_local = descend(m2m_ops, top_local, parent_c, octant_c).astype(jnp.bfloat16)
    near_b = apply_stack(m2l_ops, pack(mult_b, list_b_src, list_b_off, OFFSETS))
    b_local = (near_b + descend(m2m_ops, c_local, parent_b, octant_b)).astype(jnp.bfloat16)
    fine_result = descend(m2m_ops, b_local, parent_a, octant_a)
    return jnp.where(living[None, :], fine_result, 0.0).astype(jnp.bfloat16)
```

```python
import functools

import jax
import jax.numpy as jnp
from jax import lax
from jax.experimental import pallas as pl
from jax.experimental.pallas import tpu as pltpu
from jax.sharding import PartitionSpec as P

MESH = pl.DeviceIdType.MESH
F32 = jnp.float32
BF16 = jnp.bfloat16
I32 = jnp.int32
LANES = 128
CORES = 2


def dot(a, b, contract=(1, 0)):
    return lax.dot_general(
        a, b, (((contract[0],), (contract[1],)), ((), ())), preferred_element_type=F32
    )


def column_of(row):
    n = row.shape[1]
    diagonal = lax.broadcasted_iota(I32, (n, n), 0) == lax.broadcasted_iota(I32, (n, n), 1)
    return jnp.sum(jnp.where(diagonal, row, 0), axis=1, keepdims=True)


def kernel(
    dims,
    leaf_hbm,
    count_ref,
    pa_ref,
    oa_ref,
    pb_ref,
    ob_ref,
    pc_ref,
    oc_ref,
    lbs_ref,
    lbo_ref,
    lts_ref,
    lto_ref,
    m2m_hbm,
    m2l_hbm,
    out_ref,
    leaf_v,
    m2m_v,
    m2l_v,
    one_hot_a,
    grouped_v,
    window,
    near_t,
    pad_v,
    count_b,
    count_t,
    packed_v,
    recv1,
    send2,
    recv2,
    recv3,
    recv4,
    send5,
    recv5,
    prod_c,
    prod_b,
    load_sem,
    near_send,
    near_recv,
    send_sem,
    recv_sem,
):
    ny, nz, nx = dims
    na = CORES * nx
    k = leaf_v.shape[0]
    cells_a = leaf_v.shape[1]
    cells_b = pb_ref.shape[1]
    cells_c = pc_ref.shape[1]
    entries, tops = lts_ref.shape
    kinds = m2l_v.shape[0]
    kp = recv1.shape[1]

    leaf_i, x = lax.axis_index("leaf"), lax.axis_index("coef")
    device = leaf_i * nx + x
    devices = ny * nz * na
    core = lax.rem(leaf_i, CORES)
    z = lax.rem(leaf_i // CORES, nz)
    y = leaf_i // (CORES * nz)
    a = core * nx + x

    def at(yy, zz, aa):
        return ((yy * nz + zz) * CORES + aa // nx, lax.rem(aa, nx))

    def linear(d):
        return (d // nx, lax.rem(d, nx))

    group_a = [lax.rem(a + i, na) for i in range(1, na)]
    group_z = [lax.rem(z + i, nz) for i in range(1, nz)]
    group_y = [lax.rem(y + i, ny) for i in range(1, ny)]
    before = linear(lax.rem(device + devices - 1, devices))
    after = linear(lax.rem(device + 1, devices))

    loads = [
        pltpu.make_async_copy(leaf_hbm, leaf_v, load_sem.at[0]),
        pltpu.make_async_copy(m2m_hbm, m2m_v, load_sem.at[1]),
        pltpu.make_async_copy(m2l_hbm, m2l_v, load_sem.at[2]),
    ]
    for load in loads:
        load.start()

    barrier = pltpu.get_barrier_semaphore()
    partners = (
        [at(y, z, aa) for aa in group_a]
        + [at(y, zz, a) for zz in group_z]
        + [at(yy, z, a) for yy in group_y]
        + [before, after]
    )
    for partner in partners:
        pl.semaphore_signal(barrier, inc=1, device_id=partner, device_id_type=MESH)

    cell = (
        lax.broadcasted_iota(I32, pa_ref.shape, 0) * LANES
        + lax.broadcasted_iota(I32, pa_ref.shape, 1)
    )
    code_a = oa_ref[...] * cells_b + pa_ref[...] - device * cells_b
    code_a = jnp.where(cell < count_ref[0], code_a, -1)
    slot = lax.broadcasted_iota(I32, (8 * cells_b, LANES), 0)
    for r in range(cells_a // LANES):
        one_hot_a[:, r * LANES : (r + 1) * LANES] = (slot == code_a[r : r + 1, :]).astype(F32).astype(BF16)

    loads[0].wait()
    for o in range(8):
        rows = slice(o * cells_b, (o + 1) * cells_b)
        grouped_v[:, rows] = dot(leaf_v[...], one_hot_a[rows, :], (1, 1)).astype(BF16)
    loads[1].wait()
    mult_b = dot(m2m_v[0], grouped_v[:, :cells_b])
    for o in range(1, 8):
        mult_b = mult_b + dot(m2m_v[o], grouped_v[:, o * cells_b : (o + 1) * cells_b])
    mult_b = mult_b.astype(BF16)
    window[:, cells_b : 2 * cells_b] = jnp.zeros((window.shape[0], cells_b), BF16)
    window[0:k, cells_b : 2 * cells_b] = mult_b

    pl.semaphore_wait(barrier, len(partners))

    mine = window.at[:, cells_b : 2 * cells_b]
    to_before = pltpu.make_async_remote_copy(
        src_ref=mine,
        dst_ref=window.at[:, 2 * cells_b : 3 * cells_b],
        send_sem=near_send.at[0],
        recv_sem=near_recv.at[0],
        device_id=before,
        device_id_type=MESH,
    )
    to_after = pltpu.make_async_remote_copy(
        src_ref=mine,
        dst_ref=window.at[:, 0:cells_b],
        send_sem=near_send.at[1],
        recv_sem=near_recv.at[1],
        device_id=after,
        device_id_type=MESH,
    )
    to_before.start()
    to_after.start()

    code_b = ob_ref[...] * cells_c + pb_ref[...] - device * cells_c
    slots_b = 8 * cells_c
    one_hot_b = (lax.broadcasted_iota(I32, (slots_b, cells_b), 0) == code_b).astype(F32)
    grouped_c = dot(mult_b, one_hot_b.astype(BF16), (1, 1)).astype(BF16)
    mult_c = dot(m2m_v[0], grouped_c[:, :cells_c])
    for o in range(1, 8):
        mult_c = mult_c + dot(m2m_v[o], grouped_c[:, o * cells_c : (o + 1) * cells_c])
    octant_c = oc_ref[...]
    shifted = jnp.zeros((k, cells_c), F32)
    for o in range(8):
        shifted = shifted + dot(m2m_v[o], jnp.where(octant_c == o, mult_c, 0.0).astype(BF16))
    pad_v[...] = jnp.zeros(pad_v.shape, F32)
    pad_v[0:k, 0:cells_c] = shifted
    shifted_t = pad_v[...].T[0:cells_c, :]
    parent_c = column_of(pc_ref[...])
    octant_c = column_of(octant_c)
    lane = lax.broadcasted_iota(I32, (cells_c, kp), 1)
    message = jnp.where(
        lane == k,
        (parent_c // 32).astype(F32),
        jnp.where(lane == k + 1, (parent_c % 32).astype(F32), shifted_t),
    )

    def block(ref, i, rows):
        return ref.at[pl.ds(pl.multiple_of(i * rows, rows), rows)]

    def stage(number, partner_ids, positions, source, target, place, rows):
        copies = []
        for i, (partner, position) in enumerate(zip(partner_ids, positions)):
            src = block(target, place, rows) if source is None else block(source, position, rows)
            copy = pltpu.make_async_remote_copy(
                src_ref=src,
                dst_ref=block(target, place, rows),
                send_sem=send_sem.at[number, i],
                recv_sem=recv_sem.at[number, i],
                device_id=partner,
                device_id_type=MESH,
            )
            copy.start()
            copies.append(copy)
        return copies

    def arrive(copies):
        for copy in copies:
            copy.wait_recv()

    def total(ref, parts, rows):
        summed = ref[0:rows, :].astype(F32)
        for i in range(1, parts):
            summed = summed + ref[i * rows : (i + 1) * rows, :].astype(F32)
        return summed

    ids_a = [at(y, z, aa) for aa in group_a]
    ids_z = [at(y, zz, a) for zz in group_z]
    ids_y = [at(yy, z, a) for yy in group_y]
    rows = cells_c
    own_tops = tops // (nz * na)

    block(recv1, a, rows)[...] = message.astype(BF16)
    copies1 = stage(0, ids_a, group_a, None, recv1, a, rows)

    base = (device - 1) * cells_b
    source_id = lbs_ref[...] - base
    kind = lbo_ref[...]
    place_b = lax.broadcasted_iota(I32, (3 * cells_b, cells_b), 0)
    for o in range(kinds):
        keyed = jnp.where(kind == o, source_id, -1)
        counts = jnp.zeros((3 * cells_b, cells_b), F32)
        for e in range(entries):
            counts = counts + (place_b == keyed[e : e + 1, :]).astype(F32)
        count_b[:, o * cells_b : (o + 1) * cells_b] = counts.astype(BF16)

    arrive(copies1)
    gathered = recv1[...]
    high = gathered[:, k : k + 1].astype(F32)
    low = gathered[:, k + 1 : k + 2].astype(F32)
    parent = high * 32.0 + low
    targets = na * cells_c
    sets = nz * own_tops
    spot = lax.broadcasted_iota(I32, (targets, sets), 1)
    spot = (spot // own_tops) * (na * own_tops) + a * own_tops + spot % own_tops
    member = (parent == spot.astype(F32)).astype(F32).astype(BF16)
    send2[...] = dot(member, gathered, (0, 0)).astype(BF16)

    block(recv2, z, own_tops)[...] = block(send2, z, own_tops)[...]
    copies2 = stage(1, ids_z, group_z, send2, recv2, z, own_tops)

    listed = lto_ref[...] * tops + lts_ref[...]
    parts = jnp.concatenate([(listed // 128).astype(F32), (listed % 128).astype(F32)], axis=0)
    parent_hot = (parent == lax.broadcasted_iota(I32, (targets, tops), 1).astype(F32)).astype(F32)
    codes = dot(parts.astype(BF16), parent_hot.astype(BF16), (1, 1))
    codes = codes[0:entries, :] * 128.0 + codes[entries:, :]
    spot_t = lax.broadcasted_iota(I32, (sets, targets), 0)
    spot_t = (spot_t // own_tops) * (na * own_tops) + a * own_tops + spot_t % own_tops
    for o in range(kinds):
        wanted = (spot_t + o * tops).astype(F32)
        counts = jnp.zeros((sets, targets), F32)
        for e in range(entries):
            counts = counts + (wanted == codes[e : e + 1, :]).astype(F32)
        count_t[:, o * targets : (o + 1) * targets] = counts.astype(BF16)

    arrive(copies2)
    block(recv3, y, own_tops)[...] = total(recv2, nz, own_tops).astype(BF16)

    copies3 = stage(2, ids_y, group_y, None, recv3, y, own_tops)
    arrive(copies3)
    block(recv4, z, own_tops)[...] = total(recv3, ny, own_tops).astype(BF16)

    copies4 = stage(3, ids_z, group_z, None, recv4, z, own_tops)

    loads[2].wait()
    to_before.wait_recv()
    to_after.wait_recv()
    near = jnp.zeros((k, cells_b), F32)
    for o in range(kinds):
        packed = dot(window[0:k, :], count_b[:, o * cells_b : (o + 1) * cells_b]).astype(BF16)
        near = near + dot(m2l_v[o], packed)
    pad_v[0:k, :] = near
    near_t[...] = pad_v[...].T

    arrive(copies4)
    packed_v[...] = dot(recv4[...], count_t[...], (0, 0)).astype(BF16)
    partial = dot(m2l_v[0], packed_v[0:k, 0:targets])
    for o in range(1, kinds):
        partial = partial + dot(m2l_v[o], packed_v[0:k, o * targets : (o + 1) * targets])
    pad_v[0:k, 0:targets] = partial
    send5[...] = pad_v[...].T[0:targets, :].astype(BF16)

    block(recv5, a, rows)[...] = block(send5, a, rows)[...]
    copies5 = stage(4, ids_a, group_a, send5, recv5, a, rows)
    one_hot_bt = one_hot_b.T.astype(BF16)
    arrive(copies5)
    top_local = total(recv5, na, rows).astype(BF16)[:, 0:k]

    local_c = jnp.zeros((cells_c, k), F32)
    for o in range(8):
        local_c = local_c + jnp.where(octant_c == o, dot(top_local, m2m_v[o]), 0.0)
    local_c = local_c.astype(BF16)
    for o in range(8):
        prod_c[o * cells_c : (o + 1) * cells_c, :] = dot(local_c, m2m_v[o])
    full = prod_c[...]
    rounded = full.astype(BF16)
    rest = (full - rounded.astype(F32)).astype(BF16)
    far = dot(one_hot_bt, rounded) + dot(one_hot_bt, rest)
    local_b = (near_t[:, 0:k] + far).astype(BF16)
    for o in range(8):
        prod_b[o * cells_b : (o + 1) * cells_b, :] = dot(local_b, m2m_v[o]).astype(BF16)
    out_ref[...] = dot(prod_b[...], one_hot_a[...], (0, 0)).astype(BF16)

    to_before.wait_send()
    to_after.wait_send()
    for copy in copies1 + copies2 + copies3 + copies4 + copies5:
        copy.wait_send()


def body(dims, *args):
    (
        leaf_mult,
        fine_count,
        parent_a,
        octant_a,
        parent_b,
        octant_b,
        parent_c,
        octant_c,
        list_b_src,
        list_b_off,
        list_t_src,
        list_t_off,
        m2m_ops,
        m2l_ops,
    ) = args
    ny, nz, nx = dims
    na = CORES * nx
    k, cells_a = leaf_mult.shape
    cells_b = parent_b.shape[0]
    cells_c = parent_c.shape[0]
    tops = list_t_src.shape[0]
    kinds = m2l_ops.shape[0]
    kp = -(-(k + 2) // LANES) * LANES
    kr = -(-k // 16) * 16
    own_tops = tops // (nz * na)
    targets = na * cells_c
    sets = nz * own_tops
    wide = max(cells_b, targets)
    vmem = pl.BlockSpec(memory_space=pltpu.VMEM)
    smem = pl.BlockSpec(memory_space=pltpu.SMEM)
    hbm = pl.BlockSpec(memory_space=pl.ANY)
    most = max(na, nz, ny) - 1
    fine = pl.pallas_call(
        functools.partial(kernel, dims),
        out_shape=jax.ShapeDtypeStruct((k, cells_a), BF16),
        in_specs=[hbm, smem] + [vmem] * 10 + [hbm, hbm],
        out_specs=vmem,
        scratch_shapes=[
            pltpu.VMEM((k, cells_a), BF16),
            pltpu.VMEM(m2m_ops.shape, BF16),
            pltpu.VMEM(m2l_ops.shape, BF16),
            pltpu.VMEM((8 * cells_b, cells_a), BF16),
            pltpu.VMEM((k, 8 * cells_b), BF16),
            pltpu.VMEM((kr, 3 * cells_b), BF16),
            pltpu.VMEM((cells_b, kp), F32),
            pltpu.VMEM((kp, wide), F32),
            pltpu.VMEM((3 * cells_b, kinds * cells_b), BF16),
            pltpu.VMEM((sets, kinds * targets), BF16),
            pltpu.VMEM((kp, kinds * targets), BF16),
            pltpu.VMEM((targets, kp), BF16),
            pltpu.VMEM((sets, kp), BF16),
            pltpu.VMEM((sets, kp), BF16),
            pltpu.VMEM((ny * own_tops, kp), BF16),
            pltpu.VMEM((sets, kp), BF16),
            pltpu.VMEM((targets, kp), BF16),
            pltpu.VMEM((targets, kp), BF16),
            pltpu.VMEM((8 * cells_c, k), F32),
            pltpu.VMEM((8 * cells_b, k), BF16),
            pltpu.SemaphoreType.DMA((3,)),
            pltpu.SemaphoreType.DMA((2,)),
            pltpu.SemaphoreType.DMA((2,)),
            pltpu.SemaphoreType.DMA((5, most)),
            pltpu.SemaphoreType.DMA((5, most)),
        ],
        compiler_params=pltpu.CompilerParams(
            collective_id=0, has_side_effects=True, vmem_limit_bytes=48 * 1024 * 1024
        ),
    )(
        leaf_mult,
        fine_count,
        parent_a.reshape(-1, LANES),
        octant_a.reshape(-1, LANES),
        parent_b.reshape(1, -1),
        octant_b.reshape(1, -1),
        parent_c.reshape(1, -1),
        octant_c.reshape(1, -1),
        list_b_src.T,
        list_b_off.T,
        list_t_src.T,
        list_t_off.T,
        m2m_ops,
        m2l_ops,
    )
    return fine


def solution(mesh):
    nx = mesh.shape["coef"]
    plane = mesh.shape["leaf"] // CORES
    nz = 1
    while nz * nz < plane:
        nz *= 2
    both = P(("leaf", "coef"))
    rows = P(("leaf", "coef"), None)
    in_specs = (P(None, ("leaf", "coef")),) + (both,) * 7 + (rows, rows) + (P(),) * 4
    return jax.shard_map(
        functools.partial(body, (plane // nz, nz, nx)),
        mesh=mesh,
        in_specs=in_specs,
        out_specs=P(None, ("leaf", "coef")),
        check_vma=False,
    )
```

```python
import functools

import jax
import jax.numpy as jnp
from jax import lax
from jax.experimental import pallas as pl
from jax.experimental.pallas import tpu as pltpu
from jax.sharding import PartitionSpec as P

MESH = pl.DeviceIdType.MESH
F32 = jnp.float32
BF16 = jnp.bfloat16
I32 = jnp.int32
LANES = 128
CORES = 2


def dot(a, b, contract=(1, 0)):
    return lax.dot_general(
        a, b, (((contract[0],), (contract[1],)), ((), ())), preferred_element_type=F32
    )


def column_of(row):
    n = row.shape[1]
    diagonal = lax.broadcasted_iota(I32, (n, n), 0) == lax.broadcasted_iota(I32, (n, n), 1)
    return jnp.sum(jnp.where(diagonal, row, 0), axis=1, keepdims=True)


def kernel(
    dims,
    leaf_hbm,
    count_ref,
    pa_ref,
    oa_ref,
    pb_ref,
    ob_ref,
    pc_ref,
    oc_ref,
    lbs_ref,
    lbo_ref,
    lts_ref,
    lto_ref,
    m2m_hbm,
    m2l_hbm,
    out_ref,
    leaf_v,
    m2m_v,
    m2l_v,
    one_hot_a,
    grouped_v,
    window,
    near_t,
    pad_v,
    count_b,
    count_t,
    gathered,
    turned,
    heads,
    shares,
    arrived,
    prod_c,
    prod_b,
    load_sem,
    near_send,
    near_recv,
    sems_z,
    sems_x,
    sems_h,
    sems_q,
):
    ny, nz, nx = dims
    k = leaf_v.shape[0]
    cells_a = leaf_v.shape[1]
    cells_b = pb_ref.shape[1]
    cells_c = pc_ref.shape[1]
    entries, tops = lts_ref.shape
    kinds = m2l_v.shape[0]
    kp = gathered.shape[1]

    leaf_i, x = lax.axis_index("leaf"), lax.axis_index("coef")
    device = leaf_i * nx + x
    devices = ny * nz * CORES * nx
    core = lax.rem(leaf_i, CORES)
    z = lax.rem(leaf_i // CORES, nz)
    y = leaf_i // (CORES * nz)

    def at(dy, dz, dc, dx):
        yy, zz = lax.rem(y + dy + ny, ny), lax.rem(z + dz + nz, nz)
        cc, xx = lax.rem(core + dc + CORES, CORES), lax.rem(x + dx + nx, nx)
        return ((yy * nz + zz) * CORES + cc, xx)

    def linear(d):
        return (d // nx, lax.rem(d, nx))

    steps_z = sorted(range(nz), key=lambda i: (min(i, nz - i), i))
    steps_x = range(nx)
    steps_q = sorted(
        [(i, c) for i in range(ny) for c in range(CORES)], key=lambda s: (min(s[0], ny - s[0]), s)
    )
    before = linear(lax.rem(device + devices - 1, devices))
    after = linear(lax.rem(device + 1, devices))

    loads = [
        pltpu.make_async_copy(leaf_hbm, leaf_v, load_sem.at[0]),
        pltpu.make_async_copy(m2m_hbm, m2m_v, load_sem.at[1]),
        pltpu.make_async_copy(m2l_hbm, m2l_v, load_sem.at[2]),
    ]
    for load in loads:
        load.start()

    barrier = pltpu.get_barrier_semaphore()
    partners = (
        [at(0, j, 0, 0) for j in steps_z if j]
        + [at(0, 0, 0, i) for i in steps_x if i]
        + [at(j, 0, c, 0) for j, c in steps_q if j or c]
        + [before, after]
    )
    for partner in partners:
        pl.semaphore_signal(barrier, inc=1, device_id=partner, device_id_type=MESH)

    cell = (
        lax.broadcasted_iota(I32, pa_ref.shape, 0) * LANES
        + lax.broadcasted_iota(I32, pa_ref.shape, 1)
    )
    code_a = oa_ref[...] * cells_b + pa_ref[...] - device * cells_b
    code_a = jnp.where(cell < count_ref[0], code_a, -1)
    slot = lax.broadcasted_iota(I32, (8 * cells_b, LANES), 0)
    for r in range(cells_a // LANES):
        one_hot_a[:, r * LANES : (r + 1) * LANES] = (slot == code_a[r : r + 1, :]).astype(F32).astype(BF16)

    loads[0].wait()
    for o in range(0, 8, 2):
        rows = slice(o * cells_b, (o + 2) * cells_b)
        grouped_v[:, rows] = dot(leaf_v[...], one_hot_a[rows, :], (1, 1)).astype(BF16)
    loads[1].wait()
    mult_b = dot(m2m_v[0], grouped_v[:, :cells_b])
    for o in range(1, 8):
        mult_b = mult_b + dot(m2m_v[o], grouped_v[:, o * cells_b : (o + 1) * cells_b])
    mult_b = mult_b.astype(BF16)
    window[:, cells_b : 2 * cells_b] = jnp.zeros((window.shape[0], cells_b), BF16)
    window[0:k, cells_b : 2 * cells_b] = mult_b

    code_b = ob_ref[...] * cells_c + pb_ref[...] - device * cells_c
    slots_b = 8 * cells_c
    one_hot_b = (lax.broadcasted_iota(I32, (slots_b, cells_b), 0) == code_b).astype(F32)
    grouped_c = dot(mult_b, one_hot_b.astype(BF16), (1, 1)).astype(BF16)
    mult_c = dot(m2m_v[0], grouped_c[:, :cells_c])
    for o in range(1, 8):
        mult_c = mult_c + dot(m2m_v[o], grouped_c[:, o * cells_c : (o + 1) * cells_c])
    octant_c = oc_ref[...]
    shifted = jnp.zeros((k, cells_c), F32)
    for o in range(8):
        shifted = shifted + dot(m2m_v[o], jnp.where(octant_c == o, mult_c, 0.0).astype(BF16))
    pad_v[...] = jnp.zeros(pad_v.shape, F32)
    pad_v[0:k, 0:cells_c] = shifted
    shifted_t = pad_v[:, 0:LANES].T[0:cells_c, :]
    parent_c = column_of(pc_ref[...])
    octant_c = column_of(octant_c)
    high = (parent_c // 32).astype(F32)
    low = (parent_c % 32).astype(F32)
    lane = lax.broadcasted_iota(I32, (cells_c, kp), 1)
    message = jnp.where(lane == k, high, jnp.where(lane == k + 1, low, shifted_t))
    gathered[0:cells_c, :] = message.astype(BF16)
    lane = lax.broadcasted_iota(I32, (cells_c, LANES), 1)
    heads[0:cells_c, :] = jnp.where(lane < LANES // 2, high, low).astype(BF16)

    def send(src, dst, sems, index, partner):
        copy = pltpu.make_async_remote_copy(
            src_ref=src,
            dst_ref=dst,
            send_sem=sems[0].at[index],
            recv_sem=sems[1].at[index],
            device_id=partner,
            device_id_type=MESH,
        )
        copy.start()
        return copy

    def part(ref, i):
        return ref.at[i * cells_c : (i + 1) * cells_c]

    pl.semaphore_wait(barrier, len(partners))

    sent_z = {}
    for n, j in enumerate(steps_z):
        if j:
            sent_z[n] = send(part(gathered, 0), part(gathered, n * nx), sems_z, n - 1, at(0, j, 0, 0))
    sent_x = {}

    def spread(n):
        for i in steps_x:
            if i:
                sent_x[n, i] = send(
                    part(gathered, n * nx), part(gathered, n * nx + i), sems_x, n * (nx - 1) + i - 1, at(0, 0, 0, i)
                )

    spread(0)
    sent_heads = {}
    for n, (j, c) in enumerate(steps_q):
        if n:
            sent_heads[n] = send(part(heads, 0), part(heads, n), sems_h, n - 1, at(j, 0, c, 0))
    mine = window.at[:, cells_b : 2 * cells_b]
    near_sems = (near_send, near_recv)
    to_before = send(mine, window.at[:, 2 * cells_b : 3 * cells_b], near_sems, 0, before)
    to_after = send(mine, window.at[:, 0:cells_b], near_sems, 1, after)

    def count(place, wanted, kind, store):
        weights = []
        for first in range(0, kinds, 4):
            weight = jnp.zeros(kind.shape, I32)
            for o in range(first, min(first + 4, kinds)):
                weight = jnp.where(kind == o, 1 << (8 * (o - first)), weight)
            weights.append(weight)
        sums = [jnp.zeros((place.shape[0], kind.shape[1]), I32) for _ in weights]
        for e in range(entries):
            same = place == wanted[e : e + 1, :]
            sums = [s + jnp.where(same, w[e : e + 1, :], 0) for s, w in zip(sums, weights)]
        for o in range(kinds):
            store(o, ((sums[o // 4] >> (8 * (o % 4))) & 255).astype(F32).astype(BF16))

    def store_b(o, m):
        count_b[:, o * cells_b : (o + 1) * cells_b] = m

    place_b = lax.broadcasted_iota(I32, (3 * cells_b, cells_b), 0)
    count(place_b, lbs_ref[...] - (device - 1) * cells_b, lbo_ref[...], store_b)

    for n in range(1, nz):
        sent_z[n].wait_recv()
        spread(n)

    for n in sent_heads:
        sent_heads[n].wait_recv()
    targets = heads.shape[0]

    def parents(high, low):
        return (high.astype(F32) * 32.0 + low.astype(F32)).astype(I32)

    listed = lto_ref[...] * tops + lts_ref[...]
    split = jnp.concatenate([(listed // 128).astype(F32), (listed % 128).astype(F32)], axis=0)
    wanted = parents(heads[:, 0:1], heads[:, LANES // 2 : LANES // 2 + 1])
    wanted = (wanted == lax.broadcasted_iota(I32, (targets, tops), 1)).astype(F32)
    codes = dot(split.astype(BF16), wanted.astype(BF16), (1, 1))
    codes = (codes[0:entries, :] * 128.0 + codes[entries:, :]).astype(I32)
    source_t, kind_t = codes % tops, codes // tops

    sources = gathered.shape[0]
    chunk = min(LANES, sources)
    for first in range(0, sources, chunk):
        for n in range(first // cells_c // nx, (first + chunk) // cells_c // nx):
            for i in steps_x:
                if i:
                    sent_x[n, i].wait_recv()
        here = slice(first, first + chunk)
        place = parents(gathered[here, k : k + 1], gathered[here, k + 1 : k + 2])

        def store_t(o, m):
            count_t[here, o * targets : (o + 1) * targets] = m

        count(place, source_t, kind_t, store_t)
        turned[:, here] = gathered[here, :].T

    loads[2].wait()
    packed = dot(turned[0:k, :], count_t[:, 0:targets]).astype(BF16)
    partial = dot(m2l_v[0], packed)
    for o in range(1, kinds):
        packed = dot(turned[0:k, :], count_t[:, o * targets : (o + 1) * targets]).astype(BF16)
        partial = partial + dot(m2l_v[o], packed)
    pad_v[0:k, 0:targets] = partial
    shares[...] = pad_v[:, 0:targets].T.astype(BF16)

    sent_q = {}
    for n, (j, c) in enumerate(steps_q):
        if n:
            sent_q[n] = send(part(shares, n), part(arrived, n), sems_q, n - 1, at(-j, 0, -c, 0))

    to_before.wait_recv()
    to_after.wait_recv()
    near = jnp.zeros((k, cells_b), F32)
    for o in range(kinds):
        packed = dot(window[0:k, :], count_b[:, o * cells_b : (o + 1) * cells_b]).astype(BF16)
        near = near + dot(m2l_v[o], packed)
    pad_v[0:k, 0:cells_b] = near
    near_t[...] = pad_v[:, 0:cells_b].T
    one_hot_bt = one_hot_b.T.astype(BF16)

    top_local = shares[0:cells_c, :].astype(F32)
    for n in sent_q:
        sent_q[n].wait_recv()
    for n in sent_q:
        top_local = top_local + arrived[n * cells_c : (n + 1) * cells_c, :].astype(F32)
    top_local = top_local.astype(BF16)[:, 0:k]

    local_c = jnp.zeros((cells_c, k), F32)
    for o in range(8):
        local_c = local_c + jnp.where(octant_c == o, dot(top_local, m2m_v[o]), 0.0)
    local_c = local_c.astype(BF16)
    for o in range(8):
        prod_c[o * cells_c : (o + 1) * cells_c, :] = dot(local_c, m2m_v[o])
    full = prod_c[...]
    rounded = full.astype(BF16)
    rest = (full - rounded.astype(F32)).astype(BF16)
    far = dot(one_hot_bt, rounded) + dot(one_hot_bt, rest)
    local_b = (near_t[:, 0:k] + far).astype(BF16)
    for o in range(8):
        prod_b[o * cells_b : (o + 1) * cells_b, :] = dot(local_b, m2m_v[o]).astype(BF16)
    out_ref[...] = dot(prod_b[...], one_hot_a[...], (0, 0)).astype(BF16)

    to_before.wait_send()
    to_after.wait_send()
    for sent in (sent_z, sent_x, sent_heads, sent_q):
        for copy in sent.values():
            copy.wait_send()


def body(dims, *args):
    (
        leaf_mult,
        fine_count,
        parent_a,
        octant_a,
        parent_b,
        octant_b,
        parent_c,
        octant_c,
        list_b_src,
        list_b_off,
        list_t_src,
        list_t_off,
        m2m_ops,
        m2l_ops,
    ) = args
    ny, nz, nx = dims
    k, cells_a = leaf_mult.shape
    cells_b = parent_b.shape[0]
    cells_c = parent_c.shape[0]
    kinds = m2l_ops.shape[0]
    kp = -(-(k + 2) // LANES) * LANES
    kr = -(-k // 16) * 16
    sources = nz * nx * cells_c
    targets = ny * CORES * cells_c
    wide = max(cells_b, targets)
    vmem = pl.BlockSpec(memory_space=pltpu.VMEM)
    smem = pl.BlockSpec(memory_space=pltpu.SMEM)
    hbm = pl.BlockSpec(memory_space=pl.ANY)

    def pair(n):
        return [pltpu.SemaphoreType.DMA((n,)), pltpu.SemaphoreType.DMA((n,))]

    fine = pl.pallas_call(
        functools.partial(kernel, dims),
        out_shape=jax.ShapeDtypeStruct((k, cells_a), BF16),
        in_specs=[hbm, smem] + [vmem] * 10 + [hbm, hbm],
        out_specs=vmem,
        scratch_shapes=[
            pltpu.VMEM((k, cells_a), BF16),
            pltpu.VMEM(m2m_ops.shape, BF16),
            pltpu.VMEM(m2l_ops.shape, BF16),
            pltpu.VMEM((8 * cells_b, cells_a), BF16),
            pltpu.VMEM((k, 8 * cells_b), BF16),
            pltpu.VMEM((kr, 3 * cells_b), BF16),
            pltpu.VMEM((cells_b, kp), F32),
            pltpu.VMEM((kp, wide), F32),
            pltpu.VMEM((3 * cells_b, kinds * cells_b), BF16),
            pltpu.VMEM((sources, kinds * targets), BF16),
            pltpu.VMEM((sources, kp), BF16),
            pltpu.VMEM((kp, sources), BF16),
            pltpu.VMEM((targets, LANES), BF16),
            pltpu.VMEM((targets, kp), BF16),
            pltpu.VMEM((targets, kp), BF16),
            pltpu.VMEM((8 * cells_c, k), F32),
            pltpu.VMEM((8 * cells_b, k), BF16),
            pltpu.SemaphoreType.DMA((3,)),
            pltpu.SemaphoreType.DMA((2,)),
            pltpu.SemaphoreType.DMA((2,)),
            pair(nz - 1),
            pair(nz * (nx - 1)),
            pair(ny * CORES - 1),
            pair(ny * CORES - 1),
        ],
        compiler_params=pltpu.CompilerParams(
            collective_id=0, has_side_effects=True, vmem_limit_bytes=48 * 1024 * 1024
        ),
    )(
        leaf_mult,
        fine_count,
        parent_a.reshape(-1, LANES),
        octant_a.reshape(-1, LANES),
        parent_b.reshape(1, -1),
        octant_b.reshape(1, -1),
        parent_c.reshape(1, -1),
        octant_c.reshape(1, -1),
        list_b_src.T,
        list_b_off.T,
        list_t_src.T,
        list_t_off.T,
        m2m_ops,
        m2l_ops,
    )
    return fine


def solution(mesh):
    nx = mesh.shape["coef"]
    plane = mesh.shape["leaf"] // CORES
    nz = 1
    while nz * nz < plane:
        nz *= 2
    both = P(("leaf", "coef"))
    rows = P(("leaf", "coef"), None)
    in_specs = (P(None, ("leaf", "coef")),) + (both,) * 7 + (rows, rows) + (P(),) * 4
    return jax.shard_map(
        functools.partial(body, (plane // nz, nz, nx)),
        mesh=mesh,
        in_specs=in_specs,
        out_specs=P(None, ("leaf", "coef")),
        check_vma=False,
    )
```

```python
import functools

import jax
import jax.numpy as jnp
from jax import lax
from jax.experimental import pallas as pl
from jax.experimental.pallas import tpu as pltpu
from jax.sharding import PartitionSpec as P

MESH = pl.DeviceIdType.MESH
F32 = jnp.float32
BF16 = jnp.bfloat16
I32 = jnp.int32
LANES = 128
CORES = 2
MAIN = 256


def dot(a, b, contract=(1, 0)):
    return lax.dot_general(
        a, b, (((contract[0],), (contract[1],)), ((), ())), preferred_element_type=F32
    )


def column_of(row):
    n = row.shape[1]
    diagonal = lax.broadcasted_iota(I32, (n, n), 0) == lax.broadcasted_iota(I32, (n, n), 1)
    return jnp.sum(jnp.where(diagonal, row, 0), axis=1, keepdims=True)


def kernel(
    dims,
    leaf_hbm,
    count_ref,
    pa_ref,
    oa_ref,
    pb_ref,
    ob_ref,
    pc_ref,
    oc_ref,
    lbs_ref,
    lbo_ref,
    lts_ref,
    lto_ref,
    m2m_hbm,
    m2l_hbm,
    out_ref,
    leaf_v,
    m2m_in,
    m2l_in,
    m2m_v,
    m2m_p,
    m2l_p,
    flat,
    stack,
    one_hot_a,
    window,
    near_t,
    pad_v,
    count_b,
    count_t,
    gathered,
    turned,
    heads,
    shares,
    arrived,
    prod_c,
    prod_b,
    load_sem,
    near_send,
    near_recv,
    sems_z,
    sems_x,
    sems_h,
    sems_q,
):
    ny, nz, nx = dims
    k = leaf_v.shape[0]
    cells_a = leaf_v.shape[1]
    cells_b = pb_ref.shape[1]
    cells_c = pc_ref.shape[1]
    entries, tops = lts_ref.shape
    kinds = m2l_in.shape[1]
    rest, rest_pad = k - MAIN, (m2l_p.shape[1] - kinds * MAIN) // kinds
    kp = gathered.shape[1]

    leaf_i, x = lax.axis_index("leaf"), lax.axis_index("coef")
    device = leaf_i * nx + x
    devices = ny * nz * CORES * nx
    core = lax.rem(leaf_i, CORES)
    z = lax.rem(leaf_i // CORES, nz)
    y = leaf_i // (CORES * nz)

    def at(dy, dz, dc, dx):
        yy, zz = lax.rem(y + dy + ny, ny), lax.rem(z + dz + nz, nz)
        cc, xx = lax.rem(core + dc + CORES, CORES), lax.rem(x + dx + nx, nx)
        return ((yy * nz + zz) * CORES + cc, xx)

    def linear(d):
        return (d // nx, lax.rem(d, nx))

    steps_z = sorted(range(nz), key=lambda i: (min(i, nz - i), i))
    steps_x = range(nx)
    steps_q = sorted(
        [(i, c) for i in range(ny) for c in range(CORES)], key=lambda s: (min(s[0], ny - s[0]), s)
    )
    before = linear(lax.rem(device + devices - 1, devices))
    after = linear(lax.rem(device + 1, devices))

    loads = [
        pltpu.make_async_copy(leaf_hbm, leaf_v, load_sem.at[0]),
        pltpu.make_async_copy(m2m_hbm, m2m_in, load_sem.at[1]),
        pltpu.make_async_copy(m2l_hbm, m2l_in, load_sem.at[2]),
    ]
    for load in loads:
        load.start()

    barrier = pltpu.get_barrier_semaphore()
    partners = (
        [at(0, j, 0, 0) for j in steps_z if j]
        + [at(0, 0, 0, i) for i in steps_x if i]
        + [at(j, 0, c, 0) for j, c in steps_q if j or c]
        + [before, after]
    )
    for partner in partners:
        pl.semaphore_signal(barrier, inc=1, device_id=partner, device_id_type=MESH)

    def rest_of(o):
        return slice(kinds * MAIN + o * rest_pad, kinds * MAIN + o * rest_pad + rest)

    def separate(operators, whole, joined):
        for t in range(-(-k // LANES)):
            width = min(LANES, k - t * LANES)
            lanes = slice(t * LANES, t * LANES + width)
            flat[t, :, 0:width] = operators[:, :, lanes].astype(F32).reshape(k * kinds, width)
            for o in range(kinds):
                tile = flat.at[t][pl.ds(o, k, stride=kinds), :][:, 0:width].astype(BF16)
                if whole is not None:
                    whole[o, :, lanes] = tile
                first = t * LANES
                if first < MAIN:
                    joined[:, o * MAIN + first : o * MAIN + first + width] = tile
                else:
                    joined[:, rest_of(o)] = tile

    def put(o, value):
        n = value.shape[1]
        stack[o * MAIN : (o + 1) * MAIN, 0:n] = value[0:MAIN, :]
        stack[rest_of(o), 0:n] = value[MAIN:, :]

    stack[kinds * MAIN :, :] = jnp.zeros((kinds * rest_pad, stack.shape[1]), BF16)
    m2m_p[:, kinds * MAIN :] = jnp.zeros((k, kinds * rest_pad), BF16)
    m2l_p[:, kinds * MAIN :] = jnp.zeros((k, kinds * rest_pad), BF16)

    cell = (
        lax.broadcasted_iota(I32, pa_ref.shape, 0) * LANES
        + lax.broadcasted_iota(I32, pa_ref.shape, 1)
    )
    code_a = oa_ref[...] * cells_b + pa_ref[...] - device * cells_b
    code_a = jnp.where(cell < count_ref[0], code_a, -1)
    slot = lax.broadcasted_iota(I32, (8 * cells_b, LANES), 0)
    for r in range(cells_a // LANES):
        one_hot_a[:, r * LANES : (r + 1) * LANES] = (slot == code_a[r : r + 1, :]).astype(F32).astype(BF16)

    loads[0].wait()
    loads[1].wait()
    separate(m2m_in, m2m_v, m2m_p)
    for o in range(0, 8, 2):
        pair = dot(leaf_v[...], one_hot_a[o * cells_b : (o + 2) * cells_b, :], (1, 1)).astype(BF16)
        put(o, pair[:, :cells_b])
        put(o + 1, pair[:, cells_b:])
    mult_b = dot(m2m_p[...], stack[:, :cells_b]).astype(BF16)
    window[:, cells_b : 2 * cells_b] = jnp.zeros((window.shape[0], cells_b), BF16)
    window[0:k, cells_b : 2 * cells_b] = mult_b

    code_b = ob_ref[...] * cells_c + pb_ref[...] - device * cells_c
    slots_b = 8 * cells_c
    one_hot_b = (lax.broadcasted_iota(I32, (slots_b, cells_b), 0) == code_b).astype(F32)
    grouped_c = dot(mult_b, one_hot_b.astype(BF16), (1, 1))
    octant_of = lax.broadcasted_iota(I32, (1, slots_b), 1) // cells_c
    for o in range(8):
        put(o, jnp.where(octant_of == o, grouped_c, 0.0).astype(BF16))
    mult_c = dot(m2m_p[...], stack[:, 0:slots_b])
    turn = slots_b // 2
    while turn >= cells_c:
        mult_c = mult_c + pltpu.roll(mult_c, turn, 1)
        turn //= 2
    octant_c = oc_ref[...]
    for o in range(8):
        put(o, jnp.where(octant_c == o, mult_c[:, 0:cells_c], 0.0).astype(BF16))
    shifted = dot(m2m_p[...], stack[:, 0:cells_c])
    pad_v[...] = jnp.zeros(pad_v.shape, F32)
    pad_v[0:k, 0:cells_c] = shifted
    shifted_t = pad_v[:, 0:LANES].T[0:cells_c, :]
    parent_c = column_of(pc_ref[...])
    octant_c = column_of(octant_c)
    high = (parent_c // 32).astype(F32)
    low = (parent_c % 32).astype(F32)
    lane = lax.broadcasted_iota(I32, (cells_c, kp), 1)
    message = jnp.where(lane == k, high, jnp.where(lane == k + 1, low, shifted_t))
    gathered[0:cells_c, :] = message.astype(BF16)
    lane = lax.broadcasted_iota(I32, (cells_c, LANES), 1)
    heads[0:cells_c, :] = jnp.where(lane < LANES // 2, high, low).astype(BF16)

    def send(src, dst, sems, index, partner):
        copy = pltpu.make_async_remote_copy(
            src_ref=src,
            dst_ref=dst,
            send_sem=sems[0].at[index],
            recv_sem=sems[1].at[index],
            device_id=partner,
            device_id_type=MESH,
        )
        copy.start()
        return copy

    def part(ref, i):
        return ref.at[i * cells_c : (i + 1) * cells_c]

    pl.semaphore_wait(barrier, len(partners))

    sent_z = {}
    for n, j in enumerate(steps_z):
        if j:
            sent_z[n] = send(part(gathered, 0), part(gathered, n * nx), sems_z, n - 1, at(0, j, 0, 0))
    sent_x = {}

    def spread(n):
        for i in steps_x:
            if i:
                sent_x[n, i] = send(
                    part(gathered, n * nx), part(gathered, n * nx + i), sems_x, n * (nx - 1) + i - 1, at(0, 0, 0, i)
                )

    spread(0)
    sent_heads = {}
    for n, (j, c) in enumerate(steps_q):
        if n:
            sent_heads[n] = send(part(heads, 0), part(heads, n), sems_h, n - 1, at(j, 0, c, 0))
    mine = window.at[:, cells_b : 2 * cells_b]
    near_sems = (near_send, near_recv)
    to_before = send(mine, window.at[:, 2 * cells_b : 3 * cells_b], near_sems, 0, before)
    to_after = send(mine, window.at[:, 0:cells_b], near_sems, 1, after)

    def count(place, wanted, kind, store):
        weights = []
        for first in range(0, kinds, 4):
            weight = jnp.zeros(kind.shape, I32)
            for o in range(first, min(first + 4, kinds)):
                weight = jnp.where(kind == o, 1 << (8 * (o - first)), weight)
            weights.append(weight)
        sums = [jnp.zeros((place.shape[0], kind.shape[1]), I32) for _ in weights]
        for e in range(entries):
            same = place == wanted[e : e + 1, :]
            sums = [s + jnp.where(same, w[e : e + 1, :], 0) for s, w in zip(sums, weights)]
        for o in range(kinds):
            store(o, ((sums[o // 4] >> (8 * (o % 4))) & 255).astype(F32).astype(BF16))

    def store_b(o, m):
        count_b[:, o * cells_b : (o + 1) * cells_b] = m

    place_b = lax.broadcasted_iota(I32, (3 * cells_b, cells_b), 0)
    count(place_b, lbs_ref[...] - (device - 1) * cells_b, lbo_ref[...], store_b)

    loads[2].wait()
    separate(m2l_in, None, m2l_p)

    for n in range(1, nz):
        sent_z[n].wait_recv()
        spread(n)

    for n in sent_heads:
        sent_heads[n].wait_recv()
    targets = heads.shape[0]

    def parents(high, low):
        return (high.astype(F32) * 32.0 + low.astype(F32)).astype(I32)

    listed = lto_ref[...] * tops + lts_ref[...]
    split = jnp.concatenate([(listed // 128).astype(F32), (listed % 128).astype(F32)], axis=0)
    wanted = parents(heads[:, 0:1], heads[:, LANES // 2 : LANES // 2 + 1])
    wanted = (wanted == lax.broadcasted_iota(I32, (targets, tops), 1)).astype(F32)
    codes = dot(split.astype(BF16), wanted.astype(BF16), (1, 1))
    codes = (codes[0:entries, :] * 128.0 + codes[entries:, :]).astype(I32)
    source_t, kind_t = codes % tops, codes // tops

    sources = gathered.shape[0]
    chunk = min(LANES, sources)
    for first in range(0, sources, chunk):
        for n in range(first // cells_c // nx, (first + chunk) // cells_c // nx):
            for i in steps_x:
                if i:
                    sent_x[n, i].wait_recv()
        here = slice(first, first + chunk)
        place = parents(gathered[here, k : k + 1], gathered[here, k + 1 : k + 2])

        def store_t(o, m):
            count_t[here, o * targets : (o + 1) * targets] = m

        count(place, source_t, kind_t, store_t)
        turned[:, here] = gathered[here, :].T

    for o in range(kinds):
        put(o, dot(turned[0:k, :], count_t[:, o * targets : (o + 1) * targets]).astype(BF16))
    partial = dot(m2l_p[...], stack[:, 0:targets])
    pad_v[0:k, 0:targets] = partial
    shares[...] = pad_v[:, 0:targets].T.astype(BF16)

    sent_q = {}
    for n, (j, c) in enumerate(steps_q):
        if n:
            sent_q[n] = send(part(shares, n), part(arrived, n), sems_q, n - 1, at(-j, 0, -c, 0))

    to_before.wait_recv()
    to_after.wait_recv()
    for o in range(kinds):
        put(o, dot(window[0:k, :], count_b[:, o * cells_b : (o + 1) * cells_b]).astype(BF16))
    near = dot(m2l_p[...], stack[:, 0:cells_b])
    pad_v[0:k, 0:cells_b] = near
    near_t[...] = pad_v[:, 0:cells_b].T
    one_hot_bt = one_hot_b.T.astype(BF16)

    top_local = shares[0:cells_c, :].astype(F32)
    for n in sent_q:
        sent_q[n].wait_recv()
    for n in sent_q:
        top_local = top_local + arrived[n * cells_c : (n + 1) * cells_c, :].astype(F32)
    top_local = top_local.astype(BF16)[:, 0:k]

    local_c = jnp.zeros((cells_c, k), F32)
    for o in range(8):
        local_c = local_c + jnp.where(octant_c == o, dot(top_local, m2m_v[o]), 0.0)
    local_c = local_c.astype(BF16)
    for o in range(8):
        prod_c[o * cells_c : (o + 1) * cells_c, :] = dot(local_c, m2m_v[o])
    full = prod_c[...]
    rounded = full.astype(BF16)
    rest = (full - rounded.astype(F32)).astype(BF16)
    far = dot(one_hot_bt, rounded) + dot(one_hot_bt, rest)
    local_b = (near_t[:, 0:k] + far).astype(BF16)
    for o in range(8):
        prod_b[o * cells_b : (o + 1) * cells_b, :] = dot(local_b, m2m_v[o]).astype(BF16)
    out_ref[...] = dot(prod_b[...], one_hot_a[...], (0, 0)).astype(BF16)

    to_before.wait_send()
    to_after.wait_send()
    for sent in (sent_z, sent_x, sent_heads, sent_q):
        for copy in sent.values():
            copy.wait_send()


def body(dims, *args):
    (
        leaf_mult,
        fine_count,
        parent_a,
        octant_a,
        parent_b,
        octant_b,
        parent_c,
        octant_c,
        list_b_src,
        list_b_off,
        list_t_src,
        list_t_off,
        m2m_ops,
        m2l_ops,
    ) = args
    ny, nz, nx = dims
    k, cells_a = leaf_mult.shape
    cells_b = parent_b.shape[0]
    cells_c = parent_c.shape[0]
    kinds = m2l_ops.shape[0]
    kp = -(-(k + 2) // LANES) * LANES
    kr = -(-k // 16) * 16
    sources = nz * nx * cells_c
    targets = ny * CORES * cells_c
    wide = max(cells_b, targets)
    stacked = kinds * (MAIN + -(-(k - MAIN) // 16) * 16)
    vmem = pl.BlockSpec(memory_space=pltpu.VMEM)
    smem = pl.BlockSpec(memory_space=pltpu.SMEM)
    hbm = pl.BlockSpec(memory_space=pl.ANY)

    def pair(n):
        return [pltpu.SemaphoreType.DMA((n,)), pltpu.SemaphoreType.DMA((n,))]

    fine = pl.pallas_call(
        functools.partial(kernel, dims),
        out_shape=jax.ShapeDtypeStruct((k, cells_a), BF16),
        in_specs=[hbm, smem] + [vmem] * 10 + [hbm, hbm],
        out_specs=vmem,
        scratch_shapes=[
            pltpu.VMEM((k, cells_a), BF16),
            pltpu.VMEM((k, 8, k), BF16),
            pltpu.VMEM((k, kinds, k), BF16),
            pltpu.VMEM((8, k, k), BF16),
            pltpu.VMEM((k, stacked), BF16),
            pltpu.VMEM((k, stacked), BF16),
            pltpu.VMEM((-(-k // LANES), kinds * k, LANES), F32),
            pltpu.VMEM((stacked, wide), BF16),
            pltpu.VMEM((8 * cells_b, cells_a), BF16),
            pltpu.VMEM((kr, 3 * cells_b), BF16),
            pltpu.VMEM((cells_b, kp), F32),
            pltpu.VMEM((kp, wide), F32),
            pltpu.VMEM((3 * cells_b, kinds * cells_b), BF16),
            pltpu.VMEM((sources, kinds * targets), BF16),
            pltpu.VMEM((sources, kp), BF16),
            pltpu.VMEM((kp, sources), BF16),
            pltpu.VMEM((targets, LANES), BF16),
            pltpu.VMEM((targets, kp), BF16),
            pltpu.VMEM((targets, kp), BF16),
            pltpu.VMEM((8 * cells_c, k), F32),
            pltpu.VMEM((8 * cells_b, k), BF16),
            pltpu.SemaphoreType.DMA((3,)),
            pltpu.SemaphoreType.DMA((2,)),
            pltpu.SemaphoreType.DMA((2,)),
            pair(nz - 1),
            pair(nz * (nx - 1)),
            pair(ny * CORES - 1),
            pair(ny * CORES - 1),
        ],
        compiler_params=pltpu.CompilerParams(
            collective_id=0, has_side_effects=True, vmem_limit_bytes=56 * 1024 * 1024
        ),
    )(
        leaf_mult,
        fine_count,
        parent_a.reshape(-1, LANES),
        octant_a.reshape(-1, LANES),
        parent_b.reshape(1, -1),
        octant_b.reshape(1, -1),
        parent_c.reshape(1, -1),
        octant_c.reshape(1, -1),
        list_b_src.T,
        list_b_off.T,
        list_t_src.T,
        list_t_off.T,
        m2m_ops.transpose(1, 0, 2),
        m2l_ops.transpose(1, 0, 2),
    )
    return fine


def solution(mesh):
    nx = mesh.shape["coef"]
    plane = mesh.shape["leaf"] // CORES
    nz = 1
    while nz * nz < plane:
        nz *= 2
    both = P(("leaf", "coef"))
    rows = P(("leaf", "coef"), None)
    in_specs = (P(None, ("leaf", "coef")),) + (both,) * 7 + (rows, rows) + (P(),) * 4
    return jax.shard_map(
        functools.partial(body, (plane // nz, nz, nx)),
        mesh=mesh,
        in_specs=in_specs,
        out_specs=P(None, ("leaf", "coef")),
        check_vma=False,
    )
```

```python
import functools

import jax
import jax.numpy as jnp
from jax import lax
from jax.experimental import pallas as pl
from jax.experimental.pallas import tpu as pltpu
from jax.sharding import PartitionSpec as P

MESH = pl.DeviceIdType.MESH
F32 = jnp.float32
BF16 = jnp.bfloat16
I32 = jnp.int32
LANES = 128
CORES = 2
MAIN = 256


def dot(a, b, contract=(1, 0)):
    return lax.dot_general(
        a, b, (((contract[0],), (contract[1],)), ((), ())), preferred_element_type=F32
    )


def column_of(row):
    n = row.shape[1]
    diagonal = lax.broadcasted_iota(I32, (n, n), 0) == lax.broadcasted_iota(I32, (n, n), 1)
    return jnp.sum(jnp.where(diagonal, row, 0), axis=1, keepdims=True)


def kernel(
    dims,
    leaf_ref,
    count_ref,
    pa_ref,
    oa_ref,
    pb_ref,
    ob_ref,
    pc_ref,
    oc_ref,
    lbs_ref,
    lbo_ref,
    lts_ref,
    lto_ref,
    m2m_hbm,
    m2l_hbm,
    out_ref,
    m2m_in,
    m2l_in,
    m2m_v,
    m2m_t,
    m2m_p,
    m2l_p,
    flat,
    stack,
    one_hot_a,
    window,
    near_t,
    pad_v,
    count_b,
    count_t,
    gathered,
    turned,
    early,
    heads,
    shares,
    arrived,
    prod_c,
    prod_b,
    load_sem,
    near_send,
    near_recv,
    sems_z,
    sems_x,
    sems_h,
    sems_q,
):
    ny, nz, nx = dims
    k, cells_a = leaf_ref.shape
    cells_b = pb_ref.shape[1]
    cells_c = pc_ref.shape[1]
    entries, tops = lts_ref.shape
    kinds = m2l_in.shape[1]
    rest, rest_pad = k - MAIN, (m2l_p.shape[1] - kinds * MAIN) // kinds
    kp = gathered.shape[1]

    leaf_i, x = lax.axis_index("leaf"), lax.axis_index("coef")
    device = leaf_i * nx + x
    devices = ny * nz * CORES * nx
    core = lax.rem(leaf_i, CORES)
    z = lax.rem(leaf_i // CORES, nz)
    y = leaf_i // (CORES * nz)

    def at(dy, dz, dc, dx):
        yy, zz = lax.rem(y + dy + ny, ny), lax.rem(z + dz + nz, nz)
        cc, xx = lax.rem(core + dc + CORES, CORES), lax.rem(x + dx + nx, nx)
        return ((yy * nz + zz) * CORES + cc, xx)

    def linear(d):
        return (d // nx, lax.rem(d, nx))

    steps_z = sorted(range(nz), key=lambda i: (min(i, nz - i), i))
    steps_x = range(nx)
    steps_q = sorted(
        [(i, c) for i in range(ny) for c in range(CORES)], key=lambda s: (min(s[0], ny - s[0]), s)
    )
    before = linear(lax.rem(device + devices - 1, devices))
    after = linear(lax.rem(device + 1, devices))

    loads = [
        pltpu.make_async_copy(m2m_hbm, m2m_in, load_sem.at[0]),
        pltpu.make_async_copy(m2l_hbm, m2l_in, load_sem.at[1]),
    ]
    for load in loads:
        load.start()

    barrier = pltpu.get_barrier_semaphore()
    partners = (
        [at(0, j, 0, 0) for j in steps_z if j]
        + [at(0, 0, 0, i) for i in steps_x if i]
        + [at(j, 0, c, 0) for j, c in steps_q if j or c]
        + [before, after]
    )
    for partner in partners:
        pl.semaphore_signal(barrier, inc=1, device_id=partner, device_id_type=MESH)

    def rest_of(o):
        return slice(kinds * MAIN + o * rest_pad, kinds * MAIN + o * rest_pad + rest)

    def separate(operators, whole, joined):
        for t in range(-(-k // LANES)):
            width = min(LANES, k - t * LANES)
            lanes = slice(t * LANES, t * LANES + width)
            flat[t, :, 0:width] = operators[:, :, lanes].astype(F32).reshape(k * kinds, width)
            for o in range(kinds):
                tile = flat.at[t][pl.ds(o, k, stride=kinds), :][:, 0:width].astype(BF16)
                if whole is not None:
                    whole[o, :, lanes] = tile
                first = t * LANES
                if first < MAIN:
                    joined[:, o * MAIN + first : o * MAIN + first + width] = tile
                else:
                    joined[:, rest_of(o)] = tile

    def put(o, value):
        n = value.shape[1]
        stack[o * MAIN : (o + 1) * MAIN, 0:n] = value[0:MAIN, :]
        stack[rest_of(o), 0:n] = value[MAIN:, :]

    stack[kinds * MAIN :, :] = jnp.zeros((kinds * rest_pad, stack.shape[1]), BF16)
    m2m_p[:, kinds * MAIN :] = jnp.zeros((k, kinds * rest_pad), BF16)
    m2l_p[:, kinds * MAIN :] = jnp.zeros((k, kinds * rest_pad), BF16)

    cell = (
        lax.broadcasted_iota(I32, pa_ref.shape, 0) * LANES
        + lax.broadcasted_iota(I32, pa_ref.shape, 1)
    )
    code_a = oa_ref[...] * cells_b + pa_ref[...] - device * cells_b
    code_a = jnp.where(cell < count_ref[0], code_a, -1)
    slot = lax.broadcasted_iota(I32, (8 * cells_b, LANES), 0)
    for r in range(cells_a // LANES):
        one_hot_a[:, r * LANES : (r + 1) * LANES] = (slot == code_a[r : r + 1, :]).astype(F32).astype(BF16)

    loads[0].wait()
    separate(m2m_in, m2m_v, m2m_p)
    for o in range(8):
        m2m_t[o] = m2m_v[o].T
    for o in range(0, 8, 2):
        pair = dot(leaf_ref[...], one_hot_a[o * cells_b : (o + 2) * cells_b, :], (1, 1)).astype(BF16)
        put(o, pair[:, :cells_b])
        put(o + 1, pair[:, cells_b:])
    mult_b = dot(m2m_p[...], stack[:, :cells_b]).astype(BF16)
    window[:, cells_b : 2 * cells_b] = jnp.zeros((window.shape[0], cells_b), BF16)
    window[0:k, cells_b : 2 * cells_b] = mult_b

    code_b = ob_ref[...] * cells_c + pb_ref[...] - device * cells_c
    slots_b = 8 * cells_c
    one_hot_b = (lax.broadcasted_iota(I32, (slots_b, cells_b), 0) == code_b).astype(F32)
    grouped_c = dot(one_hot_b.astype(BF16), mult_b, (1, 1)).astype(BF16)
    mult_c = dot(grouped_c[0:cells_c, :], m2m_t[0])
    for o in range(1, 8):
        mult_c = mult_c + dot(grouped_c[o * cells_c : (o + 1) * cells_c, :], m2m_t[o])
    octant_c = column_of(oc_ref[...])
    shifted = jnp.zeros((cells_c, k), F32)
    for o in range(8):
        shifted = shifted + dot(jnp.where(octant_c == o, mult_c, 0.0).astype(BF16), m2m_t[o])
    pad_v[0:cells_c, :] = jnp.zeros((cells_c, pad_v.shape[1]), F32)
    pad_v[0:cells_c, 0:k] = shifted
    parent_c = column_of(pc_ref[...])
    high = (parent_c // 32).astype(F32)
    low = (parent_c % 32).astype(F32)
    lane = lax.broadcasted_iota(I32, (cells_c, kp), 1)
    message = jnp.where(lane == k, high, jnp.where(lane == k + 1, low, pad_v[0:cells_c, 0:kp]))
    gathered[0:cells_c, :] = message.astype(BF16)
    lane = lax.broadcasted_iota(I32, (cells_c, LANES), 1)
    heads[0:cells_c, :] = jnp.where(lane < LANES // 2, high, low).astype(BF16)

    def send(src, dst, sems, index, partner):
        copy = pltpu.make_async_remote_copy(
            src_ref=src,
            dst_ref=dst,
            send_sem=sems[0].at[index],
            recv_sem=sems[1].at[index],
            device_id=partner,
            device_id_type=MESH,
        )
        copy.start()
        return copy

    def part(ref, i):
        return ref.at[i * cells_c : (i + 1) * cells_c]

    pl.semaphore_wait(barrier, len(partners))

    sent_z = {}
    for n, j in enumerate(steps_z):
        if j:
            sent_z[n] = send(part(gathered, 0), part(gathered, n * nx), sems_z, n - 1, at(0, j, 0, 0))
    sent_x = {}

    def spread(n):
        for i in steps_x:
            if i:
                sent_x[n, i] = send(
                    part(gathered, n * nx), part(gathered, n * nx + i), sems_x, n * (nx - 1) + i - 1, at(0, 0, 0, i)
                )

    spread(0)
    sent_heads = {}
    for n, (j, c) in enumerate(steps_q):
        if n:
            sent_heads[n] = send(part(heads, 0), part(heads, n), sems_h, n - 1, at(j, 0, c, 0))
    def count(place, wanted, kind, store):
        weights = []
        for first in range(0, kinds, 4):
            weight = jnp.zeros(kind.shape, I32)
            for o in range(first, min(first + 4, kinds)):
                weight = jnp.where(kind == o, 1 << (8 * (o - first)), weight)
            weights.append(weight)
        sums = [jnp.zeros((place.shape[0], kind.shape[1]), I32) for _ in weights]
        for e in range(entries):
            same = place == wanted[e : e + 1, :]
            sums = [s + jnp.where(same, w[e : e + 1, :], 0) for s, w in zip(sums, weights)]
        for o in range(kinds):
            store(o, ((sums[o // 4] >> (8 * (o % 4))) & 255).astype(F32).astype(BF16))

    def store_b(o, m):
        count_b[:, o * cells_b : (o + 1) * cells_b] = m

    place_b = lax.broadcasted_iota(I32, (3 * cells_b, cells_b), 0)
    count(place_b, lbs_ref[...] - (device - 1) * cells_b, lbo_ref[...], store_b)

    loads[1].wait()
    separate(m2l_in, None, m2l_p)

    for n in range(1, nz):
        sent_z[n].wait_recv()
        spread(n)

    mine = window.at[:, cells_b : 2 * cells_b]
    near_sems = (near_send, near_recv)
    to_before = send(mine, window.at[:, 2 * cells_b : 3 * cells_b], near_sems, 0, before)
    to_after = send(mine, window.at[:, 0:cells_b], near_sems, 1, after)

    for n in sent_heads:
        sent_heads[n].wait_recv()
    targets = heads.shape[0]

    def parents(high, low):
        return (high.astype(F32) * 32.0 + low.astype(F32)).astype(I32)

    listed = lto_ref[...] * tops + lts_ref[...]
    split = jnp.concatenate([(listed // 128).astype(F32), (listed % 128).astype(F32)], axis=0)
    wanted = parents(heads[:, 0:1], heads[:, LANES // 2 : LANES // 2 + 1])
    wanted = (wanted == lax.broadcasted_iota(I32, (targets, tops), 1)).astype(F32)
    codes = dot(split.astype(BF16), wanted.astype(BF16), (1, 1))
    codes = (codes[0:entries, :] * 128.0 + codes[entries:, :]).astype(I32)
    source_t, kind_t = codes % tops, codes // tops

    sources = gathered.shape[0]
    half = sources // 2
    chunk = min(LANES, half)
    for first in range(0, sources, chunk):
        for n in range(first // cells_c // nx, (first + chunk) // cells_c // nx):
            for i in steps_x:
                if i:
                    sent_x[n, i].wait_recv()
        here = slice(first, first + chunk)
        place = parents(gathered[here, k : k + 1], gathered[here, k + 1 : k + 2])

        def store_t(o, m):
            count_t[here, o * targets : (o + 1) * targets] = m

        count(place, source_t, kind_t, store_t)
        turned[:, here] = gathered[here, :].T
        if first + chunk == half:
            for o in range(kinds):
                lanes = slice(o * targets, (o + 1) * targets)
                early[:, lanes] = dot(turned[0:k, 0:half], count_t[0:half, lanes])

    for o in range(kinds):
        lanes = slice(o * targets, (o + 1) * targets)
        put(o, (early[:, lanes] + dot(turned[0:k, half:], count_t[half:, lanes])).astype(BF16))
    partial = dot(m2l_p[...], stack[:, 0:targets])
    pad_v[0:k, 0:targets] = partial
    shares[...] = pad_v[:, 0:targets].T.astype(BF16)

    sent_q = {}
    for n, (j, c) in enumerate(steps_q):
        if n:
            sent_q[n] = send(part(shares, n), part(arrived, n), sems_q, n - 1, at(-j, 0, -c, 0))

    to_before.wait_recv()
    to_after.wait_recv()
    for o in range(0, kinds, 2):
        pair = dot(window[0:k, :], count_b[:, o * cells_b : (o + 2) * cells_b]).astype(BF16)
        put(o, pair[:, :cells_b])
        put(o + 1, pair[:, cells_b:])
    near = dot(m2l_p[...], stack[:, 0:cells_b])
    pad_v[0:k, 0:cells_b] = near
    near_t[...] = pad_v[:, 0:cells_b].T
    one_hot_bt = one_hot_b.T.astype(BF16)

    top_local = shares[0:cells_c, :].astype(F32)
    for n in sent_q:
        sent_q[n].wait_recv()
    for n in sent_q:
        top_local = top_local + arrived[n * cells_c : (n + 1) * cells_c, :].astype(F32)
    top_local = top_local.astype(BF16)[:, 0:k]

    local_c = jnp.zeros((cells_c, k), F32)
    for o in range(8):
        local_c = local_c + jnp.where(octant_c == o, dot(top_local, m2m_v[o]), 0.0)
    local_c = local_c.astype(BF16)
    for o in range(8):
        prod_c[o * cells_c : (o + 1) * cells_c, :] = dot(local_c, m2m_v[o])
    full = prod_c[...]
    rounded = full.astype(BF16)
    rest = (full - rounded.astype(F32)).astype(BF16)
    far = dot(one_hot_bt, rounded) + dot(one_hot_bt, rest)
    local_b = (near_t[:, 0:k] + far).astype(BF16)
    for o in range(8):
        prod_b[o * cells_b : (o + 1) * cells_b, :] = dot(local_b, m2m_v[o]).astype(BF16)
    out_ref[...] = dot(prod_b[...], one_hot_a[...], (0, 0)).astype(BF16)

    to_before.wait_send()
    to_after.wait_send()
    for sent in (sent_z, sent_x, sent_heads, sent_q):
        for copy in sent.values():
            copy.wait_send()


def body(dims, *args):
    (
        leaf_mult,
        fine_count,
        parent_a,
        octant_a,
        parent_b,
        octant_b,
        parent_c,
        octant_c,
        list_b_src,
        list_b_off,
        list_t_src,
        list_t_off,
        m2m_ops,
        m2l_ops,
    ) = args
    ny, nz, nx = dims
    k, cells_a = leaf_mult.shape
    cells_b = parent_b.shape[0]
    cells_c = parent_c.shape[0]
    kinds = m2l_ops.shape[0]
    kp = -(-(k + 2) // LANES) * LANES
    kr = -(-k // 16) * 16
    sources = nz * nx * cells_c
    targets = ny * CORES * cells_c
    wide = max(cells_b, targets)
    stacked = kinds * (MAIN + -(-(k - MAIN) // 16) * 16)
    vmem = pl.BlockSpec(memory_space=pltpu.VMEM)
    smem = pl.BlockSpec(memory_space=pltpu.SMEM)
    hbm = pl.BlockSpec(memory_space=pl.ANY)

    def pair(n):
        return [pltpu.SemaphoreType.DMA((n,)), pltpu.SemaphoreType.DMA((n,))]

    fine = pl.pallas_call(
        functools.partial(kernel, dims),
        out_shape=jax.ShapeDtypeStruct((k, cells_a), BF16),
        in_specs=[vmem, smem] + [vmem] * 10 + [hbm, hbm],
        out_specs=vmem,
        scratch_shapes=[
            pltpu.VMEM((k, 8, k), BF16),
            pltpu.VMEM((k, kinds, k), BF16),
            pltpu.VMEM((8, k, k), BF16),
            pltpu.VMEM((8, k, k), BF16),
            pltpu.VMEM((k, stacked), BF16),
            pltpu.VMEM((k, stacked), BF16),
            pltpu.VMEM((-(-k // LANES), kinds * k, LANES), F32),
            pltpu.VMEM((stacked, wide), BF16),
            pltpu.VMEM((8 * cells_b, cells_a), BF16),
            pltpu.VMEM((kr, 3 * cells_b), BF16),
            pltpu.VMEM((cells_b, kp), F32),
            pltpu.VMEM((kp, max(kp, wide)), F32),
            pltpu.VMEM((3 * cells_b, kinds * cells_b), BF16),
            pltpu.VMEM((sources, kinds * targets), BF16),
            pltpu.VMEM((sources, kp), BF16),
            pltpu.VMEM((kp, sources), BF16),
            pltpu.VMEM((k, kinds * targets), F32),
            pltpu.VMEM((targets, LANES), BF16),
            pltpu.VMEM((targets, kp), BF16),
            pltpu.VMEM((targets, kp), BF16),
            pltpu.VMEM((8 * cells_c, k), F32),
            pltpu.VMEM((8 * cells_b, k), BF16),
            pltpu.SemaphoreType.DMA((2,)),
            pltpu.SemaphoreType.DMA((2,)),
            pltpu.SemaphoreType.DMA((2,)),
            pair(nz - 1),
            pair(nz * (nx - 1)),
            pair(ny * CORES - 1),
            pair(ny * CORES - 1),
        ],
        compiler_params=pltpu.CompilerParams(
            collective_id=0, has_side_effects=True, vmem_limit_bytes=52 * 1024 * 1024
        ),
    )(
        leaf_mult,
        fine_count,
        parent_a.reshape(-1, LANES),
        octant_a.reshape(-1, LANES),
        parent_b.reshape(1, -1),
        octant_b.reshape(1, -1),
        parent_c.reshape(1, -1),
        octant_c.reshape(1, -1),
        list_b_src.T,
        list_b_off.T,
        list_t_src.T,
        list_t_off.T,
        m2m_ops.transpose(1, 0, 2),
        m2l_ops.transpose(1, 0, 2),
    )
    return fine


def solution(mesh):
    nx = mesh.shape["coef"]
    plane = mesh.shape["leaf"] // CORES
    nz = 1
    while nz * nz < plane:
        nz *= 2
    both = P(("leaf", "coef"))
    rows = P(("leaf", "coef"), None)
    in_specs = (P(None, ("leaf", "coef")),) + (both,) * 7 + (rows, rows) + (P(),) * 4
    return jax.shard_map(
        functools.partial(body, (plane // nz, nz, nx)),
        mesh=mesh,
        in_specs=in_specs,
        out_specs=P(None, ("leaf", "coef")),
        check_vma=False,
    )
```

```python
import functools

import jax
import jax.numpy as jnp
from jax import lax
from jax.experimental import pallas as pl
from jax.experimental.pallas import tpu as pltpu
from jax.sharding import PartitionSpec as P

MESH = pl.DeviceIdType.MESH
F32 = jnp.float32
BF16 = jnp.bfloat16
I32 = jnp.int32
LANES = 128
CORES = 2
MAIN = 256


def dot(a, b, contract=(1, 0)):
    return lax.dot_general(
        a, b, (((contract[0],), (contract[1],)), ((), ())), preferred_element_type=F32
    )


def column_of(row):
    n = row.shape[1]
    diagonal = lax.broadcasted_iota(I32, (n, n), 0) == lax.broadcasted_iota(I32, (n, n), 1)
    return jnp.sum(jnp.where(diagonal, row, 0), axis=1, keepdims=True)


def kernel(
    dims,
    leaf_hbm,
    count_ref,
    pa_ref,
    oa_ref,
    pb_ref,
    ob_ref,
    pc_ref,
    oc_ref,
    lbs_ref,
    lbo_ref,
    lts_ref,
    lto_ref,
    m2m_hbm,
    m2l_hbm,
    out_ref,
    leaf_ref,
    m2m_in,
    m2l_in,
    m2m_v,
    m2m_t,
    m2m_p,
    m2l_p,
    flat,
    stack,
    one_hot_a,
    window,
    near_t,
    pad_v,
    count_b,
    count_t,
    gathered,
    turned,
    early,
    heads,
    shares,
    arrived,
    prod_c,
    prod_b,
    load_sem,
    near_send,
    near_recv,
    sems_z,
    sems_x,
    sems_h,
    sems_q,
):
    ny, nz, nx = dims
    k, cells_a = leaf_ref.shape
    cells_b = pb_ref.shape[1]
    cells_c = pc_ref.shape[1]
    entries, tops = lts_ref.shape
    kinds = m2l_in.shape[1]
    rest, rest_pad = k - MAIN, (m2l_p.shape[1] - kinds * MAIN) // kinds
    kp = gathered.shape[1]

    leaf_i, x = lax.axis_index("leaf"), lax.axis_index("coef")
    device = leaf_i * nx + x
    devices = ny * nz * CORES * nx
    core = lax.rem(leaf_i, CORES)
    z = lax.rem(leaf_i // CORES, nz)
    y = leaf_i // (CORES * nz)

    def at(dy, dz, dc, dx):
        yy, zz = lax.rem(y + dy + ny, ny), lax.rem(z + dz + nz, nz)
        cc, xx = lax.rem(core + dc + CORES, CORES), lax.rem(x + dx + nx, nx)
        return ((yy * nz + zz) * CORES + cc, xx)

    def linear(d):
        return (d // nx, lax.rem(d, nx))

    steps_z = sorted(range(nz), key=lambda i: (min(i, nz - i), i))
    steps_x = range(nx)
    steps_q = sorted(
        [(i, c) for i in range(ny) for c in range(CORES)], key=lambda s: (min(s[0], ny - s[0]), s)
    )
    before = linear(lax.rem(device + devices - 1, devices))
    after = linear(lax.rem(device + 1, devices))

    loads = [
        pltpu.make_async_copy(leaf_hbm, leaf_ref, load_sem.at[2]),
        pltpu.make_async_copy(m2m_hbm, m2m_in, load_sem.at[0]),
        pltpu.make_async_copy(m2l_hbm, m2l_in, load_sem.at[1]),
    ]
    for load in loads:
        load.start()

    barrier = pltpu.get_barrier_semaphore()
    partners = (
        [at(0, j, 0, 0) for j in steps_z if j]
        + [at(0, 0, 0, i) for i in steps_x if i]
        + [at(j, 0, c, 0) for j, c in steps_q if j or c]
        + [before, after]
    )
    for partner in partners:
        pl.semaphore_signal(barrier, inc=1, device_id=partner, device_id_type=MESH)

    def rest_of(o):
        return slice(kinds * MAIN + o * rest_pad, kinds * MAIN + o * rest_pad + rest)

    def separate(operators, whole, joined):
        for t in range(-(-k // LANES)):
            width = min(LANES, k - t * LANES)
            lanes = slice(t * LANES, t * LANES + width)
            flat[t, :, 0:width] = operators[:, :, lanes].astype(F32).reshape(k * kinds, width)
            for o in range(kinds):
                tile = flat.at[t][pl.ds(o, k, stride=kinds), :][:, 0:width].astype(BF16)
                if whole is not None:
                    whole[o, :, lanes] = tile
                first = t * LANES
                if first < MAIN:
                    joined[:, o * MAIN + first : o * MAIN + first + width] = tile
                else:
                    joined[:, rest_of(o)] = tile

    def put(o, value):
        n = value.shape[1]
        stack[o * MAIN : (o + 1) * MAIN, 0:n] = value[0:MAIN, :]
        stack[rest_of(o), 0:n] = value[MAIN:, :]

    stack[kinds * MAIN :, :] = jnp.zeros((kinds * rest_pad, stack.shape[1]), BF16)
    m2m_p[:, kinds * MAIN :] = jnp.zeros((k, kinds * rest_pad), BF16)
    m2l_p[:, kinds * MAIN :] = jnp.zeros((k, kinds * rest_pad), BF16)

    cell = (
        lax.broadcasted_iota(I32, pa_ref.shape, 0) * LANES
        + lax.broadcasted_iota(I32, pa_ref.shape, 1)
    )
    code_a = oa_ref[...] * cells_b + pa_ref[...] - device * cells_b
    code_a = jnp.where(cell < count_ref[...], code_a, -1)
    slot = lax.broadcasted_iota(I32, (8 * cells_b, LANES), 0)
    for r in range(cells_a // LANES):
        one_hot_a[:, r * LANES : (r + 1) * LANES] = (slot == code_a[r : r + 1, :]).astype(F32).astype(BF16)

    loads[0].wait()
    loads[1].wait()
    separate(m2m_in, m2m_v, m2m_p)
    for o in range(8):
        m2m_t[o] = m2m_v[o].T
    for o in range(0, 8, 2):
        pair = dot(leaf_ref[...], one_hot_a[o * cells_b : (o + 2) * cells_b, :], (1, 1)).astype(BF16)
        put(o, pair[:, :cells_b])
        put(o + 1, pair[:, cells_b:])
    mult_b = dot(m2m_p[...], stack[:, :cells_b]).astype(BF16)
    window[:, cells_b : 2 * cells_b] = jnp.zeros((window.shape[0], cells_b), BF16)
    window[0:k, cells_b : 2 * cells_b] = mult_b

    code_b = ob_ref[...] * cells_c + pb_ref[...] - device * cells_c
    slots_b = 8 * cells_c
    one_hot_b = (lax.broadcasted_iota(I32, (slots_b, cells_b), 0) == code_b).astype(F32)
    grouped_c = dot(one_hot_b.astype(BF16), mult_b, (1, 1)).astype(BF16)
    mult_c = dot(grouped_c[0:cells_c, :], m2m_t[0])
    for o in range(1, 8):
        mult_c = mult_c + dot(grouped_c[o * cells_c : (o + 1) * cells_c, :], m2m_t[o])
    octant_c = column_of(oc_ref[...])
    shifted = jnp.zeros((cells_c, k), F32)
    for o in range(8):
        shifted = shifted + dot(jnp.where(octant_c == o, mult_c, 0.0).astype(BF16), m2m_t[o])
    pad_v[0:cells_c, :] = jnp.zeros((cells_c, pad_v.shape[1]), F32)
    pad_v[0:cells_c, 0:k] = shifted
    parent_c = column_of(pc_ref[...])
    high = (parent_c // 32).astype(F32)
    low = (parent_c % 32).astype(F32)
    lane = lax.broadcasted_iota(I32, (cells_c, kp), 1)
    message = jnp.where(lane == k, high, jnp.where(lane == k + 1, low, pad_v[0:cells_c, 0:kp]))
    gathered[0:cells_c, :] = message.astype(BF16)
    lane = lax.broadcasted_iota(I32, (cells_c, LANES), 1)
    heads[0:cells_c, :] = jnp.where(lane < LANES // 2, high, low).astype(BF16)

    def send(src, dst, sems, index, partner):
        copy = pltpu.make_async_remote_copy(
            src_ref=src,
            dst_ref=dst,
            send_sem=sems[0].at[index],
            recv_sem=sems[1].at[index],
            device_id=partner,
            device_id_type=MESH,
        )
        copy.start()
        return copy

    def part(ref, i):
        return ref.at[i * cells_c : (i + 1) * cells_c]

    pl.semaphore_wait(barrier, len(partners))

    sent_z = {}
    for n, j in enumerate(steps_z):
        if j:
            sent_z[n] = send(part(gathered, 0), part(gathered, n * nx), sems_z, n - 1, at(0, j, 0, 0))
    sent_x = {}

    def spread(n):
        for i in steps_x:
            if i:
                sent_x[n, i] = send(
                    part(gathered, n * nx), part(gathered, n * nx + i), sems_x, n * (nx - 1) + i - 1, at(0, 0, 0, i)
                )

    spread(0)
    sent_heads = {}
    for n, (j, c) in enumerate(steps_q):
        if n:
            sent_heads[n] = send(part(heads, 0), part(heads, n), sems_h, n - 1, at(j, 0, c, 0))
    def count(place, wanted, kind, store):
        weights = []
        for first in range(0, kinds, 4):
            weight = jnp.zeros(kind.shape, I32)
            for o in range(first, min(first + 4, kinds)):
                weight = jnp.where(kind == o, 1 << (8 * (o - first)), weight)
            weights.append(weight)
        sums = [jnp.zeros((place.shape[0], kind.shape[1]), I32) for _ in weights]
        for e in range(entries):
            same = place == wanted[e : e + 1, :]
            sums = [s + jnp.where(same, w[e : e + 1, :], 0) for s, w in zip(sums, weights)]
        for o in range(kinds):
            store(o, ((sums[o // 4] >> (8 * (o % 4))) & 255).astype(F32).astype(BF16))

    def store_b(o, m):
        count_b[:, o * cells_b : (o + 1) * cells_b] = m

    place_b = lax.broadcasted_iota(I32, (3 * cells_b, cells_b), 0)
    count(place_b, lbs_ref[...] - (device - 1) * cells_b, lbo_ref[...], store_b)

    loads[2].wait()
    separate(m2l_in, None, m2l_p)

    for n in range(1, nz):
        sent_z[n].wait_recv()
        spread(n)

    mine = window.at[:, cells_b : 2 * cells_b]
    near_sems = (near_send, near_recv)
    to_before = send(mine, window.at[:, 2 * cells_b : 3 * cells_b], near_sems, 0, before)
    to_after = send(mine, window.at[:, 0:cells_b], near_sems, 1, after)

    for n in sent_heads:
        sent_heads[n].wait_recv()
    targets = heads.shape[0]

    def parents(high, low):
        return (high.astype(F32) * 32.0 + low.astype(F32)).astype(I32)

    listed = lto_ref[...] * tops + lts_ref[...]
    split = jnp.concatenate([(listed // 128).astype(F32), (listed % 128).astype(F32)], axis=0)
    wanted = parents(heads[:, 0:1], heads[:, LANES // 2 : LANES // 2 + 1])
    wanted = (wanted == lax.broadcasted_iota(I32, (targets, tops), 1)).astype(F32)
    codes = dot(split.astype(BF16), wanted.astype(BF16), (1, 1))
    codes = (codes[0:entries, :] * 128.0 + codes[entries:, :]).astype(I32)
    source_t, kind_t = codes % tops, codes // tops

    sources = gathered.shape[0]
    half = sources // 2
    chunk = min(LANES, half)
    for first in range(0, sources, chunk):
        for n in range(first // cells_c // nx, (first + chunk) // cells_c // nx):
            for i in steps_x:
                if i:
                    sent_x[n, i].wait_recv()
        here = slice(first, first + chunk)
        place = parents(gathered[here, k : k + 1], gathered[here, k + 1 : k + 2])

        def store_t(o, m):
            count_t[here, o * targets : (o + 1) * targets] = m

        count(place, source_t, kind_t, store_t)
        turned[:, here] = gathered[here, :].T
        if first + chunk == half:
            for o in range(kinds):
                lanes = slice(o * targets, (o + 1) * targets)
                early[:, lanes] = dot(turned[0:k, 0:half], count_t[0:half, lanes])

    for o in range(kinds):
        lanes = slice(o * targets, (o + 1) * targets)
        put(o, (early[:, lanes] + dot(turned[0:k, half:], count_t[half:, lanes])).astype(BF16))
    partial = dot(m2l_p[...], stack[:, 0:targets])
    pad_v[0:k, 0:targets] = partial
    shares[...] = pad_v[:, 0:targets].T.astype(BF16)

    sent_q = {}
    for n, (j, c) in enumerate(steps_q):
        if n:
            sent_q[n] = send(part(shares, n), part(arrived, n), sems_q, n - 1, at(-j, 0, -c, 0))

    to_before.wait_recv()
    to_after.wait_recv()
    for o in range(0, kinds, 2):
        pair = dot(window[0:k, :], count_b[:, o * cells_b : (o + 2) * cells_b]).astype(BF16)
        put(o, pair[:, :cells_b])
        put(o + 1, pair[:, cells_b:])
    near = dot(m2l_p[...], stack[:, 0:cells_b])
    pad_v[0:k, 0:cells_b] = near
    near_t[...] = pad_v[:, 0:cells_b].T
    one_hot_bt = one_hot_b.T.astype(BF16)

    top_local = shares[0:cells_c, :].astype(F32)
    for n in sent_q:
        sent_q[n].wait_recv()
    for n in sent_q:
        top_local = top_local + arrived[n * cells_c : (n + 1) * cells_c, :].astype(F32)
    top_local = top_local.astype(BF16)[:, 0:k]

    local_c = jnp.zeros((cells_c, k), F32)
    for o in range(8):
        local_c = local_c + jnp.where(octant_c == o, dot(top_local, m2m_v[o]), 0.0)
    local_c = local_c.astype(BF16)
    for o in range(8):
        prod_c[o * cells_c : (o + 1) * cells_c, :] = dot(local_c, m2m_v[o])
    full = prod_c[...]
    rounded = full.astype(BF16)
    rest = (full - rounded.astype(F32)).astype(BF16)
    far = dot(one_hot_bt, rounded) + dot(one_hot_bt, rest)
    local_b = (near_t[:, 0:k] + far).astype(BF16)
    for o in range(8):
        prod_b[o * cells_b : (o + 1) * cells_b, :] = dot(local_b, m2m_v[o]).astype(BF16)
    out_ref[...] = dot(prod_b[...], one_hot_a[...], (0, 0)).astype(BF16)

    to_before.wait_send()
    to_after.wait_send()
    for sent in (sent_z, sent_x, sent_heads, sent_q):
        for copy in sent.values():
            copy.wait_send()


def body(dims, *args):
    (
        leaf_mult,
        fine_count,
        parent_a,
        octant_a,
        parent_b,
        octant_b,
        parent_c,
        octant_c,
        list_b_src,
        list_b_off,
        list_t_src,
        list_t_off,
        m2m_ops,
        m2l_ops,
    ) = args
    ny, nz, nx = dims
    k, cells_a = leaf_mult.shape
    cells_b = parent_b.shape[0]
    cells_c = parent_c.shape[0]
    kinds = m2l_ops.shape[0]
    kp = -(-(k + 2) // LANES) * LANES
    kr = -(-k // 16) * 16
    sources = nz * nx * cells_c
    targets = ny * CORES * cells_c
    wide = max(cells_b, targets)
    stacked = kinds * (MAIN + -(-(k - MAIN) // 16) * 16)
    vmem = pl.BlockSpec(memory_space=pltpu.VMEM)
    hbm = pl.BlockSpec(memory_space=pl.ANY)

    def here(array):
        return pltpu.with_memory_space_constraint(array, pltpu.HBM)

    def pair(n):
        return [pltpu.SemaphoreType.DMA((n,)), pltpu.SemaphoreType.DMA((n,))]

    fine = pl.pallas_call(
        functools.partial(kernel, dims),
        out_shape=pltpu.VMEM((k, cells_a), BF16),
        in_specs=[hbm] + [vmem] * 11 + [hbm, hbm],
        out_specs=vmem,
        scratch_shapes=[
            pltpu.VMEM((k, cells_a), BF16),
            pltpu.VMEM((k, 8, k), BF16),
            pltpu.VMEM((k, kinds, k), BF16),
            pltpu.VMEM((8, k, k), BF16),
            pltpu.VMEM((8, k, k), BF16),
            pltpu.VMEM((k, stacked), BF16),
            pltpu.VMEM((k, stacked), BF16),
            pltpu.VMEM((-(-k // LANES), kinds * k, LANES), F32),
            pltpu.VMEM((stacked, wide), BF16),
            pltpu.VMEM((8 * cells_b, cells_a), BF16),
            pltpu.VMEM((kr, 3 * cells_b), BF16),
            pltpu.VMEM((cells_b, kp), F32),
            pltpu.VMEM((kp, max(kp, wide)), F32),
            pltpu.VMEM((3 * cells_b, kinds * cells_b), BF16),
            pltpu.VMEM((sources, kinds * targets), BF16),
            pltpu.VMEM((sources, kp), BF16),
            pltpu.VMEM((kp, sources), BF16),
            pltpu.VMEM((k, kinds * targets), F32),
            pltpu.VMEM((targets, LANES), BF16),
            pltpu.VMEM((targets, kp), BF16),
            pltpu.VMEM((targets, kp), BF16),
            pltpu.VMEM((8 * cells_c, k), F32),
            pltpu.VMEM((8 * cells_b, k), BF16),
            pltpu.SemaphoreType.DMA((3,)),
            pltpu.SemaphoreType.DMA((2,)),
            pltpu.SemaphoreType.DMA((2,)),
            pair(nz - 1),
            pair(nz * (nx - 1)),
            pair(ny * CORES - 1),
            pair(ny * CORES - 1),
        ],
        compiler_params=pltpu.CompilerParams(
            collective_id=0, has_side_effects=True, vmem_limit_bytes=52 * 1024 * 1024
        ),
    )(
        here(leaf_mult),
        fine_count.reshape(1, 1),
        here(parent_a.reshape(-1, LANES)),
        here(octant_a.reshape(-1, LANES)),
        here(parent_b.reshape(1, -1)),
        here(octant_b.reshape(1, -1)),
        here(parent_c.reshape(1, -1)),
        here(octant_c.reshape(1, -1)),
        here(list_b_src.T),
        here(list_b_off.T),
        here(list_t_src.T),
        here(list_t_off.T),
        here(m2m_ops.transpose(1, 0, 2)),
        here(m2l_ops.transpose(1, 0, 2)),
    )
    return fine


def solution(mesh):
    nx = mesh.shape["coef"]
    plane = mesh.shape["leaf"] // CORES
    nz = 1
    while nz * nz < plane:
        nz *= 2
    both = P(("leaf", "coef"))
    rows = P(("leaf", "coef"), None)
    in_specs = (P(None, ("leaf", "coef")),) + (both,) * 7 + (rows, rows) + (P(),) * 4
    return jax.shard_map(
        functools.partial(body, (plane // nz, nz, nx)),
        mesh=mesh,
        in_specs=in_specs,
        out_specs=P(None, ("leaf", "coef")),
        check_vma=False,
    )
```

```python
import functools

import jax
import jax.numpy as jnp
from jax import lax
from jax.experimental import pallas as pl
from jax.experimental.pallas import tpu as pltpu
from jax.sharding import PartitionSpec as P

MESH = pl.DeviceIdType.MESH
F32 = jnp.float32
BF16 = jnp.bfloat16
I32 = jnp.int32
LANES = 128
CORES = 2
MAIN = 256


def dot(a, b, contract=(1, 0)):
    return lax.dot_general(
        a, b, (((contract[0],), (contract[1],)), ((), ())), preferred_element_type=F32
    )


def stacked_dot(operator, stack):
    cut = operator.shape[0] // 32 * 16
    return jnp.concatenate([dot(operator[0:cut, :], stack), dot(operator[cut:, :], stack)], axis=0)


def column_of(row):
    n = row.shape[1]
    diagonal = lax.broadcasted_iota(I32, (n, n), 0) == lax.broadcasted_iota(I32, (n, n), 1)
    return jnp.sum(jnp.where(diagonal, row, 0), axis=1, keepdims=True)


def kernel(
    dims,
    leaf_hbm,
    count_ref,
    pa_hbm,
    oa_hbm,
    pb_hbm,
    ob_hbm,
    pc_hbm,
    oc_hbm,
    lbs_hbm,
    lbo_hbm,
    lts_hbm,
    lto_hbm,
    m2m_hbm,
    m2l_hbm,
    out_ref,
    pa_ref,
    oa_ref,
    pb_ref,
    ob_ref,
    pc_ref,
    oc_ref,
    lbs_ref,
    lbo_ref,
    lts_ref,
    lto_ref,
    leaf_ref,
    m2m_in,
    m2l_in,
    m2m_v,
    m2m_t,
    m2m_p,
    m2l_p,
    flat,
    stack,
    one_hot_a,
    window,
    near_t,
    pad_v,
    count_b,
    count_t,
    gathered,
    turned,
    early,
    heads,
    shares,
    arrived,
    prod_c,
    prod_b,
    load_sem,
    near_send,
    near_recv,
    sems_z,
    sems_x,
    sems_h,
    sems_q,
):
    ny, nz, nx = dims
    k, cells_a = leaf_ref.shape
    cells_b = pb_ref.shape[1]
    cells_c = pc_ref.shape[1]
    entries, tops = lts_ref.shape
    kinds = m2l_in.shape[1]
    rest, rest_pad = k - MAIN, (m2l_p.shape[1] - kinds * MAIN) // kinds
    kp = gathered.shape[1]

    leaf_i, x = lax.axis_index("leaf"), lax.axis_index("coef")
    device = leaf_i * nx + x
    devices = ny * nz * CORES * nx
    core = lax.rem(leaf_i, CORES)
    z = lax.rem(leaf_i // CORES, nz)
    y = leaf_i // (CORES * nz)

    def at(dy, dz, dc, dx):
        yy, zz = lax.rem(y + dy + ny, ny), lax.rem(z + dz + nz, nz)
        cc, xx = lax.rem(core + dc + CORES, CORES), lax.rem(x + dx + nx, nx)
        return ((yy * nz + zz) * CORES + cc, xx)

    def linear(d):
        return (d // nx, lax.rem(d, nx))

    steps_z = sorted(range(nz), key=lambda i: (min(i, nz - i), i))
    steps_x = range(nx)
    direct = [n for n, j in enumerate(steps_z) if min(j, nz - j) == 1]
    steps_q = sorted(
        [(i, c) for i in range(ny) for c in range(CORES)], key=lambda s: (min(s[0], ny - s[0]), s)
    )
    before = linear(lax.rem(device + devices - 1, devices))
    after = linear(lax.rem(device + 1, devices))

    loads = [
        pltpu.make_async_copy(leaf_hbm, leaf_ref, load_sem.at[2]),
        pltpu.make_async_copy(m2m_hbm, m2m_in, load_sem.at[0]),
        pltpu.make_async_copy(m2l_hbm, m2l_in, load_sem.at[1]),
    ]
    index_refs = (
        (pa_hbm, pa_ref),
        (oa_hbm, oa_ref),
        (pb_hbm, pb_ref),
        (ob_hbm, ob_ref),
        (pc_hbm, pc_ref),
        (oc_hbm, oc_ref),
        (lbs_hbm, lbs_ref),
        (lbo_hbm, lbo_ref),
        (lts_hbm, lts_ref),
        (lto_hbm, lto_ref),
    )
    indices = [
        pltpu.make_async_copy(src, dst, load_sem.at[3 + i]) for i, (src, dst) in enumerate(index_refs)
    ]
    for load in indices[0:2] + loads[0:2]:
        load.start()

    barrier = pltpu.get_barrier_semaphore()
    partners = (
        [at(0, j, 0, 0) for j in steps_z if j]
        + [at(0, 0, 0, i) for i in steps_x if i]
        + [at(0, steps_z[n], 0, i) for n in direct for i in steps_x if i]
        + [at(j, 0, c, 0) for j, c in steps_q if j or c]
        + [before, after]
    )
    for partner in partners:
        pl.semaphore_signal(barrier, inc=1, device_id=partner, device_id_type=MESH)
    for load in indices[2:]:
        load.start()

    def rest_of(o):
        return slice(kinds * MAIN + o * rest_pad, kinds * MAIN + o * rest_pad + rest)

    def separate(operators, whole, joined):
        for t in range(-(-k // LANES)):
            width = min(LANES, k - t * LANES)
            lanes = slice(t * LANES, t * LANES + width)
            flat[t, :, 0:width] = operators[:, :, lanes].astype(F32).reshape(k * kinds, width)
            for o in range(kinds):
                tile = flat.at[t][pl.ds(o, k, stride=kinds), :][:, 0:width].astype(BF16)
                if whole is not None:
                    whole[o, :, lanes] = tile
                first = t * LANES
                if first < MAIN:
                    joined[:, o * MAIN + first : o * MAIN + first + width] = tile
                else:
                    joined[:, rest_of(o)] = tile

    def put(o, value):
        n = value.shape[1]
        stack[o * MAIN : (o + 1) * MAIN, 0:n] = value[0:MAIN, :]
        stack[rest_of(o), 0:n] = value[MAIN:, :]

    stack[kinds * MAIN :, :] = jnp.zeros((kinds * rest_pad, stack.shape[1]), BF16)
    m2m_p[:, kinds * MAIN :] = jnp.zeros((k, kinds * rest_pad), BF16)
    m2l_p[:, kinds * MAIN :] = jnp.zeros((k, kinds * rest_pad), BF16)

    indices[0].wait()
    indices[1].wait()
    cell = (
        lax.broadcasted_iota(I32, pa_ref.shape, 0) * LANES
        + lax.broadcasted_iota(I32, pa_ref.shape, 1)
    )
    code_a = oa_ref[...] * cells_b + pa_ref[...] - device * cells_b
    code_a = jnp.where(cell < count_ref[0], code_a, -1)
    slot = lax.broadcasted_iota(I32, (8 * cells_b, LANES), 0)
    for r in range(cells_a // LANES):
        one_hot_a[:, r * LANES : (r + 1) * LANES] = (slot == code_a[r : r + 1, :]).astype(F32).astype(BF16)

    for load in loads[0:2] + indices[2:]:
        load.wait()
    loads[2].start()
    separate(m2m_in, m2m_v, m2m_p)
    for o in range(0, 8, 2):
        pair = dot(leaf_ref[...], one_hot_a[o * cells_b : (o + 2) * cells_b, :], (1, 1)).astype(BF16)
        put(o, pair[:, :cells_b])
        put(o + 1, pair[:, cells_b:])
        m2m_t[o] = m2m_v[o].T
        m2m_t[o + 1] = m2m_v[o + 1].T
    mult_b = stacked_dot(m2m_p, stack[:, :cells_b]).astype(BF16)
    window[:, cells_b : 2 * cells_b] = jnp.zeros((window.shape[0], cells_b), BF16)
    window[0:k, cells_b : 2 * cells_b] = mult_b

    code_b = ob_ref[...] * cells_c + pb_ref[...] - device * cells_c
    slots_b = 8 * cells_c
    one_hot_b = (lax.broadcasted_iota(I32, (slots_b, cells_b), 0) == code_b).astype(F32)
    grouped_c = dot(one_hot_b.astype(BF16), mult_b, (1, 1)).astype(BF16)
    mult_c = dot(grouped_c[0:cells_c, :], m2m_t[0])
    for o in range(1, 8):
        mult_c = mult_c + dot(grouped_c[o * cells_c : (o + 1) * cells_c, :], m2m_t[o])
    octant_c = column_of(oc_ref[...])
    shifted = jnp.zeros((cells_c, k), F32)
    for o in range(8):
        shifted = shifted + dot(jnp.where(octant_c == o, mult_c, 0.0).astype(BF16), m2m_t[o])
    pad_v[0:cells_c, :] = jnp.zeros((cells_c, pad_v.shape[1]), F32)
    pad_v[0:cells_c, 0:k] = shifted
    parent_c = column_of(pc_ref[...])
    high = (parent_c // 32).astype(F32)
    low = (parent_c % 32).astype(F32)
    lane = lax.broadcasted_iota(I32, (cells_c, kp), 1)
    message = jnp.where(lane == k, high, jnp.where(lane == k + 1, low, pad_v[0:cells_c, 0:kp]))
    gathered[0:cells_c, :] = message.astype(BF16)
    lane = lax.broadcasted_iota(I32, (cells_c, LANES), 1)
    heads[0:cells_c, :] = jnp.where(lane < LANES // 2, high, low).astype(BF16)

    def send(src, dst, sems, index, partner):
        copy = pltpu.make_async_remote_copy(
            src_ref=src,
            dst_ref=dst,
            send_sem=sems[0].at[index],
            recv_sem=sems[1].at[index],
            device_id=partner,
            device_id_type=MESH,
        )
        copy.start()
        return copy

    def part(ref, i):
        return ref.at[i * cells_c : (i + 1) * cells_c]

    pl.semaphore_wait(barrier, len(partners))

    sent_z, sent_x = {}, {}

    def along_x(n, source, dz):
        for i in steps_x:
            if i:
                sent_x[n, i] = send(
                    part(gathered, source), part(gathered, n * nx + i), sems_x, n * (nx - 1) + i - 1, at(0, dz, 0, i)
                )

    for n in reversed(range(1, nz)):
        sent_z[n] = send(part(gathered, 0), part(gathered, n * nx), sems_z, n - 1, at(0, steps_z[n], 0, 0))
        if n in direct:
            along_x(n, 0, steps_z[n])
    along_x(0, 0, 0)
    sent_heads = {}
    for n, (j, c) in enumerate(steps_q):
        if n:
            sent_heads[n] = send(part(heads, 0), part(heads, n), sems_h, n - 1, at(j, 0, c, 0))
    def count(place, wanted, kind, store):
        weights = []
        for first in range(0, kinds, 4):
            weight = jnp.zeros(kind.shape, I32)
            for o in range(first, min(first + 4, kinds)):
                weight = jnp.where(kind == o, 1 << (8 * (o - first)), weight)
            weights.append(weight)
        sums = [jnp.zeros((place.shape[0], kind.shape[1]), I32) for _ in weights]
        for e in range(entries):
            same = place == wanted[e : e + 1, :]
            sums = [s + jnp.where(same, w[e : e + 1, :], 0) for s, w in zip(sums, weights)]
        for o in range(kinds):
            store(o, ((sums[o // 4] >> (8 * (o % 4))) & 255).astype(F32).astype(BF16))

    def store_b(o, m):
        count_b[:, o * cells_b : (o + 1) * cells_b] = m

    place_b = lax.broadcasted_iota(I32, (3 * cells_b, cells_b), 0)
    count(place_b, lbs_ref[...] - (device - 1) * cells_b, lbo_ref[...], store_b)

    loads[2].wait()
    separate(m2l_in, None, m2l_p)

    for n in range(1, nz):
        if n not in direct:
            sent_z[n].wait_recv()
            along_x(n, n * nx, 0)

    mine = window.at[:, cells_b : 2 * cells_b]
    near_sems = (near_send, near_recv)
    to_before = send(mine, window.at[:, 2 * cells_b : 3 * cells_b], near_sems, 0, before)
    to_after = send(mine, window.at[:, 0:cells_b], near_sems, 1, after)

    for n in sent_heads:
        sent_heads[n].wait_recv()
    targets = heads.shape[0]

    def parents(high, low):
        return (high.astype(F32) * 32.0 + low.astype(F32)).astype(I32)

    listed = lto_ref[...] * tops + lts_ref[...]
    split = jnp.concatenate([(listed // 128).astype(F32), (listed % 128).astype(F32)], axis=0)
    wanted = parents(heads[:, 0:1], heads[:, LANES // 2 : LANES // 2 + 1])
    wanted = (wanted == lax.broadcasted_iota(I32, (targets, tops), 1)).astype(F32)
    codes = dot(split.astype(BF16), wanted.astype(BF16), (1, 1))
    codes = (codes[0:entries, :] * 128.0 + codes[entries:, :]).astype(I32)
    source_t, kind_t = codes % tops, codes // tops

    sources = gathered.shape[0]
    half = sources // 2
    chunk = min(LANES, half)
    for first in range(0, sources, chunk):
        for n in range(first // cells_c // nx, (first + chunk) // cells_c // nx):
            if n in direct:
                sent_z[n].wait_recv()
            for i in steps_x:
                if i:
                    sent_x[n, i].wait_recv()
        here = slice(first, first + chunk)
        place = parents(gathered[here, k : k + 1], gathered[here, k + 1 : k + 2])

        def store_t(o, m):
            count_t[here, o * targets : (o + 1) * targets] = m

        count(place, source_t, kind_t, store_t)
        turned[:, here] = gathered[here, :].T
        if first + chunk == half:
            for o in range(kinds):
                lanes = slice(o * targets, (o + 1) * targets)
                early[:, lanes] = dot(turned[0:k, 0:half], count_t[0:half, lanes])

    for o in range(kinds):
        lanes = slice(o * targets, (o + 1) * targets)
        put(o, (early[:, lanes] + dot(turned[0:k, half:], count_t[half:, lanes])).astype(BF16))
    partial = stacked_dot(m2l_p, stack[:, 0:targets])
    pad_v[0:k, 0:targets] = partial
    shares[...] = pad_v[:, 0:targets].T.astype(BF16)

    sent_q = {}
    for n, (j, c) in enumerate(steps_q):
        if n:
            sent_q[n] = send(part(shares, n), part(arrived, n), sems_q, n - 1, at(-j, 0, -c, 0))

    to_before.wait_recv()
    to_after.wait_recv()
    for o in range(0, kinds, 2):
        pair = dot(window[0:k, :], count_b[:, o * cells_b : (o + 2) * cells_b]).astype(BF16)
        put(o, pair[:, :cells_b])
        put(o + 1, pair[:, cells_b:])
    near = stacked_dot(m2l_p, stack[:, 0:cells_b])
    pad_v[0:k, 0:cells_b] = near
    near_t[...] = pad_v[:, 0:cells_b].T
    one_hot_bt = one_hot_b.T.astype(BF16)

    top_local = shares[0:cells_c, :].astype(F32)
    for n in sent_q:
        sent_q[n].wait_recv()
    for n in sent_q:
        top_local = top_local + arrived[n * cells_c : (n + 1) * cells_c, :].astype(F32)
    top_local = top_local.astype(BF16)[:, 0:k]

    local_c = jnp.zeros((cells_c, k), F32)
    for o in range(8):
        local_c = local_c + jnp.where(octant_c == o, dot(top_local, m2m_v[o]), 0.0)
    local_c = local_c.astype(BF16)
    for o in range(8):
        prod_c[o * cells_c : (o + 1) * cells_c, :] = dot(local_c, m2m_v[o])
    full = prod_c[...]
    rounded = full.astype(BF16)
    rest = (full - rounded.astype(F32)).astype(BF16)
    far = dot(one_hot_bt, rounded) + dot(one_hot_bt, rest)
    local_b = (near_t[:, 0:k] + far).astype(BF16)
    for o in range(8):
        prod_b[o * cells_b : (o + 1) * cells_b, :] = dot(local_b, m2m_v[o]).astype(BF16)
    out_ref[...] = dot(prod_b[...], one_hot_a[...], (0, 0)).astype(BF16)

    to_before.wait_send()
    to_after.wait_send()
    for sent in (sent_z, sent_x, sent_heads, sent_q):
        for copy in sent.values():
            copy.wait_send()


def body(dims, *args):
    (
        leaf_mult,
        fine_count,
        parent_a,
        octant_a,
        parent_b,
        octant_b,
        parent_c,
        octant_c,
        list_b_src,
        list_b_off,
        list_t_src,
        list_t_off,
        m2m_ops,
        m2l_ops,
    ) = args
    ny, nz, nx = dims
    k, cells_a = leaf_mult.shape
    cells_b = parent_b.shape[0]
    cells_c = parent_c.shape[0]
    kinds = m2l_ops.shape[0]
    kp = -(-(k + 2) // LANES) * LANES
    kr = -(-k // 16) * 16
    sources = nz * nx * cells_c
    targets = ny * CORES * cells_c
    wide = max(cells_b, targets)
    stacked = kinds * (MAIN + -(-(k - MAIN) // 16) * 16)
    vmem = pl.BlockSpec(memory_space=pltpu.VMEM)
    smem = pl.BlockSpec(memory_space=pltpu.SMEM)
    hbm = pl.BlockSpec(memory_space=pl.ANY)

    def here(array):
        return pltpu.with_memory_space_constraint(array, pltpu.HBM)

    def pair(n):
        return [pltpu.SemaphoreType.DMA((n,)), pltpu.SemaphoreType.DMA((n,))]

    fine = pl.pallas_call(
        functools.partial(kernel, dims),
        out_shape=pltpu.VMEM((k, cells_a), BF16),
        in_specs=[hbm, smem] + [hbm] * 10 + [hbm, hbm],
        out_specs=vmem,
        scratch_shapes=[
            pltpu.VMEM((cells_a // LANES, LANES), I32),
            pltpu.VMEM((cells_a // LANES, LANES), I32),
            pltpu.VMEM((1, cells_b), I32),
            pltpu.VMEM((1, cells_b), I32),
            pltpu.VMEM((1, cells_c), I32),
            pltpu.VMEM((1, cells_c), I32),
            pltpu.VMEM(list_b_src.shape[::-1], I32),
            pltpu.VMEM(list_b_src.shape[::-1], I32),
            pltpu.VMEM(list_t_src.shape[::-1], I32),
            pltpu.VMEM(list_t_src.shape[::-1], I32),
            pltpu.VMEM((k, cells_a), BF16),
            pltpu.VMEM((k, 8, k), BF16),
            pltpu.VMEM((k, kinds, k), BF16),
            pltpu.VMEM((8, k, k), BF16),
            pltpu.VMEM((8, k, k), BF16),
            pltpu.VMEM((k, stacked), BF16),
            pltpu.VMEM((k, stacked), BF16),
            pltpu.VMEM((-(-k // LANES), kinds * k, LANES), F32),
            pltpu.VMEM((stacked, wide), BF16),
            pltpu.VMEM((8 * cells_b, cells_a), BF16),
            pltpu.VMEM((kr, 3 * cells_b), BF16),
            pltpu.VMEM((cells_b, kp), F32),
            pltpu.VMEM((kp, max(kp, wide)), F32),
            pltpu.VMEM((3 * cells_b, kinds * cells_b), BF16),
            pltpu.VMEM((sources, kinds * targets), BF16),
            pltpu.VMEM((sources, kp), BF16),
            pltpu.VMEM((kp, sources), BF16),
            pltpu.VMEM((k, kinds * targets), F32),
            pltpu.VMEM((targets, LANES), BF16),
            pltpu.VMEM((targets, kp), BF16),
            pltpu.VMEM((targets, kp), BF16),
            pltpu.VMEM((8 * cells_c, k), F32),
            pltpu.VMEM((8 * cells_b, k), BF16),
            pltpu.SemaphoreType.DMA((13,)),
            pltpu.SemaphoreType.DMA((2,)),
            pltpu.SemaphoreType.DMA((2,)),
            pair(nz - 1),
            pair(nz * (nx - 1)),
            pair(ny * CORES - 1),
            pair(ny * CORES - 1),
        ],
        compiler_params=pltpu.CompilerParams(
            collective_id=0, has_side_effects=True, vmem_limit_bytes=52 * 1024 * 1024
        ),
    )(
        here(leaf_mult),
        fine_count,
        here(parent_a.reshape(-1, LANES)),
        here(octant_a.reshape(-1, LANES)),
        here(parent_b.reshape(1, -1)),
        here(octant_b.reshape(1, -1)),
        here(parent_c.reshape(1, -1)),
        here(octant_c.reshape(1, -1)),
        here(list_b_src.T),
        here(list_b_off.T),
        here(list_t_src.T),
        here(list_t_off.T),
        here(m2m_ops.transpose(1, 0, 2)),
        here(m2l_ops.transpose(1, 0, 2)),
    )
    return fine


def solution(mesh):
    nx = mesh.shape["coef"]
    plane = mesh.shape["leaf"] // CORES
    nz = 1
    while nz * nz < plane:
        nz *= 2
    both = P(("leaf", "coef"))
    rows = P(("leaf", "coef"), None)
    in_specs = (P(None, ("leaf", "coef")),) + (both,) * 7 + (rows, rows) + (P(),) * 4
    return jax.shard_map(
        functools.partial(body, (plane // nz, nz, nx)),
        mesh=mesh,
        in_specs=in_specs,
        out_specs=P(None, ("leaf", "coef")),
        check_vma=False,
    )
```

```python
import functools

import jax
import jax.numpy as jnp
from jax import lax
from jax.experimental import pallas as pl
from jax.experimental.pallas import tpu as pltpu
from jax.sharding import PartitionSpec as P

MESH = pl.DeviceIdType.MESH
F32 = jnp.float32
BF16 = jnp.bfloat16
I32 = jnp.int32
LANES = 128
CORES = 2
MAIN = 256


def dot(a, b, contract=(1, 0)):
    return lax.dot_general(
        a, b, (((contract[0],), (contract[1],)), ((), ())), preferred_element_type=F32
    )


def stacked_dot(operator, stack):
    cut = operator.shape[0] // 32 * 16
    return jnp.concatenate([dot(operator[0:cut, :], stack), dot(operator[cut:, :], stack)], axis=0)


def column_of(row):
    n = row.shape[1]
    diagonal = lax.broadcasted_iota(I32, (n, n), 0) == lax.broadcasted_iota(I32, (n, n), 1)
    return jnp.sum(jnp.where(diagonal, row, 0), axis=1, keepdims=True)


def kernel(
    dims,
    leaf_hbm,
    count_ref,
    pa_hbm,
    oa_hbm,
    pb_hbm,
    ob_hbm,
    pc_hbm,
    oc_hbm,
    lbs_hbm,
    lbo_hbm,
    lts_hbm,
    lto_hbm,
    m2m_hbm,
    m2l_hbm,
    out_ref,
    pa_ref,
    oa_ref,
    pb_ref,
    ob_ref,
    pc_ref,
    oc_ref,
    lbs_ref,
    lbo_ref,
    lts_ref,
    lto_ref,
    leaf_ref,
    m2m_in,
    m2l_in,
    m2m_v,
    m2m_t,
    m2m_p,
    m2l_p,
    flat,
    stack,
    one_hot_a,
    window,
    near_t,
    pad_v,
    count_b,
    count_t,
    gathered,
    turned,
    early,
    heads,
    shares,
    arrived,
    prod_c,
    prod_b,
    load_sem,
    near_send,
    near_recv,
    sems_z,
    sems_x,
    sems_h,
    sems_q,
):
    ny, nz, nx = dims
    k, cells_a = leaf_ref.shape
    cells_b = pb_ref.shape[1]
    cells_c = pc_ref.shape[1]
    entries, tops = lts_ref.shape
    kinds = m2l_in.shape[1]
    rest, rest_pad = k - MAIN, (m2l_p.shape[1] - kinds * MAIN) // kinds
    kp = gathered.shape[1]

    leaf_i, x = lax.axis_index("leaf"), lax.axis_index("coef")
    device = leaf_i * nx + x
    devices = ny * nz * CORES * nx
    core = lax.rem(leaf_i, CORES)
    z = lax.rem(leaf_i // CORES, nz)
    y = leaf_i // (CORES * nz)

    def at(dy, dz, dc, dx):
        yy, zz = lax.rem(y + dy + ny, ny), lax.rem(z + dz + nz, nz)
        cc, xx = lax.rem(core + dc + CORES, CORES), lax.rem(x + dx + nx, nx)
        return ((yy * nz + zz) * CORES + cc, xx)

    def linear(d):
        return (d // nx, lax.rem(d, nx))

    steps_z = sorted(range(nz), key=lambda i: (min(i, nz - i), i))
    steps_x = sorted(range(nx), key=lambda i: (-min(i, nx - i), i))
    direct = [n for n, j in enumerate(steps_z) if min(j, nz - j) == 1]
    steps_q = sorted(
        [(i, c) for i in range(ny) for c in range(CORES)], key=lambda s: (min(s[0], ny - s[0]), s)
    )
    before = linear(lax.rem(device + devices - 1, devices))
    after = linear(lax.rem(device + 1, devices))

    loads = [
        pltpu.make_async_copy(leaf_hbm, leaf_ref, load_sem.at[2]),
        pltpu.make_async_copy(m2m_hbm, m2m_in, load_sem.at[0]),
        pltpu.make_async_copy(m2l_hbm, m2l_in, load_sem.at[1]),
    ]
    index_refs = (
        (pa_hbm, pa_ref),
        (oa_hbm, oa_ref),
        (pb_hbm, pb_ref),
        (ob_hbm, ob_ref),
        (pc_hbm, pc_ref),
        (oc_hbm, oc_ref),
        (lbs_hbm, lbs_ref),
        (lbo_hbm, lbo_ref),
        (lts_hbm, lts_ref),
        (lto_hbm, lto_ref),
    )
    indices = [
        pltpu.make_async_copy(src, dst, load_sem.at[3 + i]) for i, (src, dst) in enumerate(index_refs)
    ]
    for load in indices[0:2] + loads[0:2]:
        load.start()

    barrier = pltpu.get_barrier_semaphore()
    partners = (
        [at(0, j, 0, 0) for j in steps_z if j]
        + [at(0, 0, 0, i) for i in steps_x if i]
        + [at(0, steps_z[n], 0, i) for n in direct for i in steps_x if i]
        + [at(j, 0, c, 0) for j, c in steps_q if j or c]
        + [before, after]
    )
    for partner in partners:
        pl.semaphore_signal(barrier, inc=1, device_id=partner, device_id_type=MESH)
    for load in indices[2:]:
        load.start()

    def rest_of(o):
        return slice(kinds * MAIN + o * rest_pad, kinds * MAIN + o * rest_pad + rest)

    def separate(operators, whole, joined):
        for t in range(-(-k // LANES)):
            width = min(LANES, k - t * LANES)
            lanes = slice(t * LANES, t * LANES + width)
            flat[t, :, 0:width] = operators[:, :, lanes].astype(F32).reshape(k * kinds, width)
            for o in range(kinds):
                tile = flat.at[t][pl.ds(o, k, stride=kinds), :][:, 0:width].astype(BF16)
                if whole is not None:
                    whole[o, :, lanes] = tile
                first = t * LANES
                if first < MAIN:
                    joined[:, o * MAIN + first : o * MAIN + first + width] = tile
                else:
                    joined[:, rest_of(o)] = tile

    def put(o, value):
        n = value.shape[1]
        stack[o * MAIN : (o + 1) * MAIN, 0:n] = value[0:MAIN, :]
        stack[rest_of(o), 0:n] = value[MAIN:, :]

    stack[kinds * MAIN :, :] = jnp.zeros((kinds * rest_pad, stack.shape[1]), BF16)
    m2m_p[:, kinds * MAIN :] = jnp.zeros((k, kinds * rest_pad), BF16)
    m2l_p[:, kinds * MAIN :] = jnp.zeros((k, kinds * rest_pad), BF16)

    indices[0].wait()
    indices[1].wait()
    cell = (
        lax.broadcasted_iota(I32, pa_ref.shape, 0) * LANES
        + lax.broadcasted_iota(I32, pa_ref.shape, 1)
    )
    code_a = oa_ref[...] * cells_b + pa_ref[...] - device * cells_b
    code_a = jnp.where(cell < count_ref[0], code_a, -1)
    slot = lax.broadcasted_iota(I32, (8 * cells_b, LANES), 0)
    for r in range(cells_a // LANES):
        one_hot_a[:, r * LANES : (r + 1) * LANES] = (slot == code_a[r : r + 1, :]).astype(F32).astype(BF16)

    for load in loads[0:2] + indices[2:]:
        load.wait()
    loads[2].start()
    separate(m2m_in, m2m_v, m2m_p)
    for o in range(0, 8, 2):
        pair = dot(leaf_ref[...], one_hot_a[o * cells_b : (o + 2) * cells_b, :], (1, 1)).astype(BF16)
        put(o, pair[:, :cells_b])
        put(o + 1, pair[:, cells_b:])
        m2m_t[o] = m2m_v[o].T
        m2m_t[o + 1] = m2m_v[o + 1].T
    mult_b = stacked_dot(m2m_p, stack[:, :cells_b]).astype(BF16)
    window[:, cells_b : 2 * cells_b] = jnp.zeros((window.shape[0], cells_b), BF16)
    window[0:k, cells_b : 2 * cells_b] = mult_b

    code_b = ob_ref[...] * cells_c + pb_ref[...] - device * cells_c
    slots_b = 8 * cells_c
    one_hot_b = (lax.broadcasted_iota(I32, (slots_b, cells_b), 0) == code_b).astype(F32)
    grouped_c = dot(one_hot_b.astype(BF16), mult_b, (1, 1)).astype(BF16)
    mult_c = dot(grouped_c[0:cells_c, :], m2m_t[0])
    for o in range(1, 8):
        mult_c = mult_c + dot(grouped_c[o * cells_c : (o + 1) * cells_c, :], m2m_t[o])
    octant_c = column_of(oc_ref[...])
    shifted = jnp.zeros((cells_c, k), F32)
    for o in range(8):
        shifted = shifted + dot(jnp.where(octant_c == o, mult_c, 0.0).astype(BF16), m2m_t[o])
    pad_v[0:cells_c, :] = jnp.zeros((cells_c, pad_v.shape[1]), F32)
    pad_v[0:cells_c, 0:k] = shifted
    parent_c = column_of(pc_ref[...])
    high = (parent_c // 32).astype(F32)
    low = (parent_c % 32).astype(F32)
    lane = lax.broadcasted_iota(I32, (cells_c, kp), 1)
    message = jnp.where(lane == k, high, jnp.where(lane == k + 1, low, pad_v[0:cells_c, 0:kp]))
    gathered[0:cells_c, :] = message.astype(BF16)
    lane = lax.broadcasted_iota(I32, (cells_c, LANES), 1)
    heads[0:cells_c, :] = jnp.where(lane < LANES // 2, high, low).astype(BF16)

    def send(src, dst, sems, index, partner):
        copy = pltpu.make_async_remote_copy(
            src_ref=src,
            dst_ref=dst,
            send_sem=sems[0].at[index],
            recv_sem=sems[1].at[index],
            device_id=partner,
            device_id_type=MESH,
        )
        copy.start()
        return copy

    def part(ref, i):
        return ref.at[i * cells_c : (i + 1) * cells_c]

    pl.semaphore_wait(barrier, len(partners))

    sent_z, sent_x = {}, {}

    def along_x(n, source, dz):
        for i in steps_x:
            if i:
                sent_x[n, i] = send(
                    part(gathered, source), part(gathered, n * nx + i), sems_x, n * (nx - 1) + i - 1, at(0, dz, 0, i)
                )

    for n in reversed(range(1, nz)):
        sent_z[n] = send(part(gathered, 0), part(gathered, n * nx), sems_z, n - 1, at(0, steps_z[n], 0, 0))
        if n in direct:
            along_x(n, 0, steps_z[n])
    along_x(0, 0, 0)
    far_first = list(reversed(list(enumerate(steps_q))))
    sent_heads = {}
    for n, (j, c) in far_first:
        if n:
            sent_heads[n] = send(part(heads, 0), part(heads, n), sems_h, n - 1, at(j, 0, c, 0))
    def count(place, wanted, kind, store):
        weights = []
        for first in range(0, kinds, 4):
            weight = jnp.zeros(kind.shape, I32)
            for o in range(first, min(first + 4, kinds)):
                weight = jnp.where(kind == o, 1 << (8 * (o - first)), weight)
            weights.append(weight)
        sums = [jnp.zeros((place.shape[0], kind.shape[1]), I32) for _ in weights]
        for e in range(entries):
            same = place == wanted[e : e + 1, :]
            sums = [s + jnp.where(same, w[e : e + 1, :], 0) for s, w in zip(sums, weights)]
        for o in range(kinds):
            store(o, ((sums[o // 4] >> (8 * (o % 4))) & 255).astype(F32).astype(BF16))

    def store_b(o, m):
        count_b[:, o * cells_b : (o + 1) * cells_b] = m

    place_b = lax.broadcasted_iota(I32, (3 * cells_b, cells_b), 0)
    count(place_b, lbs_ref[...] - (device - 1) * cells_b, lbo_ref[...], store_b)

    loads[2].wait()
    separate(m2l_in, None, m2l_p)

    for n in range(1, nz):
        if n not in direct:
            sent_z[n].wait_recv()
            along_x(n, n * nx, 0)

    mine = window.at[:, cells_b : 2 * cells_b]
    near_sems = (near_send, near_recv)
    to_before = send(mine, window.at[:, 2 * cells_b : 3 * cells_b], near_sems, 0, before)
    to_after = send(mine, window.at[:, 0:cells_b], near_sems, 1, after)

    for n in sent_heads:
        sent_heads[n].wait_recv()
    targets = heads.shape[0]

    def parents(high, low):
        return (high.astype(F32) * 32.0 + low.astype(F32)).astype(I32)

    listed = lto_ref[...] * tops + lts_ref[...]
    split = jnp.concatenate([(listed // 128).astype(F32), (listed % 128).astype(F32)], axis=0)
    wanted = parents(heads[:, 0:1], heads[:, LANES // 2 : LANES // 2 + 1])
    wanted = (wanted == lax.broadcasted_iota(I32, (targets, tops), 1)).astype(F32)
    codes = dot(split.astype(BF16), wanted.astype(BF16), (1, 1))
    codes = (codes[0:entries, :] * 128.0 + codes[entries:, :]).astype(I32)
    source_t, kind_t = codes % tops, codes // tops

    sources = gathered.shape[0]
    half = sources // 2
    chunk = min(LANES, half)
    for first in range(0, sources, chunk):
        for n in range(first // cells_c // nx, (first + chunk) // cells_c // nx):
            if n in direct:
                sent_z[n].wait_recv()
            for i in steps_x:
                if i:
                    sent_x[n, i].wait_recv()
        here = slice(first, first + chunk)
        place = parents(gathered[here, k : k + 1], gathered[here, k + 1 : k + 2])

        def store_t(o, m):
            count_t[here, o * targets : (o + 1) * targets] = m

        count(place, source_t, kind_t, store_t)
        turned[:, here] = gathered[here, :].T
        if first + chunk == half:
            for o in range(kinds):
                lanes = slice(o * targets, (o + 1) * targets)
                early[:, lanes] = dot(turned[0:k, 0:half], count_t[0:half, lanes])

    for o in range(kinds):
        lanes = slice(o * targets, (o + 1) * targets)
        put(o, (early[:, lanes] + dot(turned[0:k, half:], count_t[half:, lanes])).astype(BF16))
    partial = stacked_dot(m2l_p, stack[:, 0:targets])
    pad_v[0:k, 0:targets] = partial
    shares[...] = pad_v[:, 0:targets].T.astype(BF16)

    sent_q = {}
    for n, (j, c) in far_first:
        if n:
            sent_q[n] = send(part(shares, n), part(arrived, n), sems_q, n - 1, at(-j, 0, -c, 0))

    to_before.wait_recv()
    to_after.wait_recv()
    for o in range(0, kinds, 2):
        pair = dot(window[0:k, :], count_b[:, o * cells_b : (o + 2) * cells_b]).astype(BF16)
        put(o, pair[:, :cells_b])
        put(o + 1, pair[:, cells_b:])
    near = stacked_dot(m2l_p, stack[:, 0:cells_b])
    pad_v[0:k, 0:cells_b] = near
    near_t[...] = pad_v[:, 0:cells_b].T
    one_hot_bt = one_hot_b.T.astype(BF16)

    top_local = shares[0:cells_c, :].astype(F32)
    for n in sent_q:
        sent_q[n].wait_recv()
    for n in sent_q:
        top_local = top_local + arrived[n * cells_c : (n + 1) * cells_c, :].astype(F32)
    top_local = top_local.astype(BF16)[:, 0:k]

    local_c = jnp.zeros((cells_c, k), F32)
    for o in range(8):
        local_c = local_c + jnp.where(octant_c == o, dot(top_local, m2m_v[o]), 0.0)
    local_c = local_c.astype(BF16)
    for o in range(8):
        prod_c[o * cells_c : (o + 1) * cells_c, :] = dot(local_c, m2m_v[o])
    full = prod_c[...]
    rounded = full.astype(BF16)
    rest = (full - rounded.astype(F32)).astype(BF16)
    far = dot(one_hot_bt, rounded) + dot(one_hot_bt, rest)
    local_b = (near_t[:, 0:k] + far).astype(BF16)
    for o in range(8):
        prod_b[o * cells_b : (o + 1) * cells_b, :] = dot(local_b, m2m_v[o]).astype(BF16)
    out_ref[...] = dot(prod_b[...], one_hot_a[...], (0, 0)).astype(BF16)

    to_before.wait_send()
    to_after.wait_send()
    for sent in (sent_z, sent_x, sent_heads, sent_q):
        for copy in sent.values():
            copy.wait_send()


def body(dims, *args):
    (
        leaf_mult,
        fine_count,
        parent_a,
        octant_a,
        parent_b,
        octant_b,
        parent_c,
        octant_c,
        list_b_src,
        list_b_off,
        list_t_src,
        list_t_off,
        m2m_ops,
        m2l_ops,
    ) = args
    ny, nz, nx = dims
    k, cells_a = leaf_mult.shape
    cells_b = parent_b.shape[0]
    cells_c = parent_c.shape[0]
    kinds = m2l_ops.shape[0]
    kp = -(-(k + 2) // LANES) * LANES
    kr = -(-k // 16) * 16
    sources = nz * nx * cells_c
    targets = ny * CORES * cells_c
    wide = max(cells_b, targets)
    stacked = kinds * (MAIN + -(-(k - MAIN) // 16) * 16)
    vmem = pl.BlockSpec(memory_space=pltpu.VMEM)
    smem = pl.BlockSpec(memory_space=pltpu.SMEM)
    hbm = pl.BlockSpec(memory_space=pl.ANY)

    def here(array):
        return pltpu.with_memory_space_constraint(array, pltpu.HBM)

    def pair(n):
        return [pltpu.SemaphoreType.DMA((n,)), pltpu.SemaphoreType.DMA((n,))]

    fine = pl.pallas_call(
        functools.partial(kernel, dims),
        out_shape=pltpu.VMEM((k, cells_a), BF16),
        in_specs=[hbm, smem] + [hbm] * 10 + [hbm, hbm],
        out_specs=vmem,
        scratch_shapes=[
            pltpu.VMEM((cells_a // LANES, LANES), I32),
            pltpu.VMEM((cells_a // LANES, LANES), I32),
            pltpu.VMEM((1, cells_b), I32),
            pltpu.VMEM((1, cells_b), I32),
            pltpu.VMEM((1, cells_c), I32),
            pltpu.VMEM((1, cells_c), I32),
            pltpu.VMEM(list_b_src.shape[::-1], I32),
            pltpu.VMEM(list_b_src.shape[::-1], I32),
            pltpu.VMEM(list_t_src.shape[::-1], I32),
            pltpu.VMEM(list_t_src.shape[::-1], I32),
            pltpu.VMEM((k, cells_a), BF16),
            pltpu.VMEM((k, 8, k), BF16),
            pltpu.VMEM((k, kinds, k), BF16),
            pltpu.VMEM((8, k, k), BF16),
            pltpu.VMEM((8, k, k), BF16),
            pltpu.VMEM((k, stacked), BF16),
            pltpu.VMEM((k, stacked), BF16),
            pltpu.VMEM((-(-k // LANES), kinds * k, LANES), F32),
            pltpu.VMEM((stacked, wide), BF16),
            pltpu.VMEM((8 * cells_b, cells_a), BF16),
            pltpu.VMEM((kr, 3 * cells_b), BF16),
            pltpu.VMEM((cells_b, kp), F32),
            pltpu.VMEM((kp, max(kp, wide)), F32),
            pltpu.VMEM((3 * cells_b, kinds * cells_b), BF16),
            pltpu.VMEM((sources, kinds * targets), BF16),
            pltpu.VMEM((sources, kp), BF16),
            pltpu.VMEM((kp, sources), BF16),
            pltpu.VMEM((k, kinds * targets), F32),
            pltpu.VMEM((targets, LANES), BF16),
            pltpu.VMEM((targets, kp), BF16),
            pltpu.VMEM((targets, kp), BF16),
            pltpu.VMEM((8 * cells_c, k), F32),
            pltpu.VMEM((8 * cells_b, k), BF16),
            pltpu.SemaphoreType.DMA((13,)),
            pltpu.SemaphoreType.DMA((2,)),
            pltpu.SemaphoreType.DMA((2,)),
            pair(nz - 1),
            pair(nz * (nx - 1)),
            pair(ny * CORES - 1),
            pair(ny * CORES - 1),
        ],
        compiler_params=pltpu.CompilerParams(
            collective_id=0, has_side_effects=True, vmem_limit_bytes=52 * 1024 * 1024
        ),
    )(
        here(leaf_mult),
        fine_count,
        here(parent_a.reshape(-1, LANES)),
        here(octant_a.reshape(-1, LANES)),
        here(parent_b.reshape(1, -1)),
        here(octant_b.reshape(1, -1)),
        here(parent_c.reshape(1, -1)),
        here(octant_c.reshape(1, -1)),
        here(list_b_src.T),
        here(list_b_off.T),
        here(list_t_src.T),
        here(list_t_off.T),
        here(m2m_ops.transpose(1, 0, 2)),
        here(m2l_ops.transpose(1, 0, 2)),
    )
    return fine


def solution(mesh):
    nx = mesh.shape["coef"]
    plane = mesh.shape["leaf"] // CORES
    nz = 1
    while nz * nz < plane:
        nz *= 2
    both = P(("leaf", "coef"))
    rows = P(("leaf", "coef"), None)
    in_specs = (P(None, ("leaf", "coef")),) + (both,) * 7 + (rows, rows) + (P(),) * 4
    return jax.shard_map(
        functools.partial(body, (plane // nz, nz, nx)),
        mesh=mesh,
        in_specs=in_specs,
        out_specs=P(None, ("leaf", "coef")),
        check_vma=False,
    )
```

```python
import functools

import jax
import jax.numpy as jnp
from jax import lax
from jax.experimental import pallas as pl
from jax.experimental.pallas import tpu as pltpu
from jax.sharding import PartitionSpec as P

MESH = pl.DeviceIdType.MESH
F32 = jnp.float32
BF16 = jnp.bfloat16
I32 = jnp.int32
LANES = 128
CORES = 2
MAIN = 256


def dot(a, b, contract=(1, 0)):
    return lax.dot_general(
        a, b, (((contract[0],), (contract[1],)), ((), ())), preferred_element_type=F32
    )


def stacked_dot(operator, stack):
    cut = operator.shape[0] // 32 * 16
    return jnp.concatenate([dot(operator[0:cut, :], stack), dot(operator[cut:, :], stack)], axis=0)


def column_of(row):
    n = row.shape[1]
    diagonal = lax.broadcasted_iota(I32, (n, n), 0) == lax.broadcasted_iota(I32, (n, n), 1)
    return jnp.sum(jnp.where(diagonal, row, 0), axis=1, keepdims=True)


def kernel(
    dims,
    leaf_hbm,
    count_ref,
    pa_hbm,
    oa_hbm,
    pb_hbm,
    ob_hbm,
    pc_hbm,
    oc_hbm,
    lbs_hbm,
    lbo_hbm,
    lts_hbm,
    lto_hbm,
    m2m_hbm,
    m2l_hbm,
    out_ref,
    pa_ref,
    oa_ref,
    pb_ref,
    ob_ref,
    pc_ref,
    oc_ref,
    lbs_ref,
    lbo_ref,
    lts_ref,
    lto_ref,
    leaf_ref,
    m2m_in,
    m2l_in,
    m2m_v,
    m2m_t,
    m2m_p,
    m2l_p,
    flat,
    stack,
    one_hot_a,
    window,
    near_t,
    pad_v,
    count_b,
    count_t,
    gathered,
    turned,
    early,
    heads,
    shares,
    arrived,
    prod_c,
    prod_b,
    load_sem,
    near_send,
    near_recv,
    sems_z,
    sems_x,
    sems_h,
    sems_q,
):
    ny, nz, nx = dims
    k, cells_a = leaf_ref.shape
    cells_b = pb_ref.shape[1]
    cells_c = pc_ref.shape[1]
    entries, tops = lts_ref.shape
    kinds = m2l_in.shape[1]
    rest, rest_pad = k - MAIN, (m2l_p.shape[1] - kinds * MAIN) // kinds
    kp = gathered.shape[1]

    leaf_i, x = lax.axis_index("leaf"), lax.axis_index("coef")
    device = leaf_i * nx + x
    devices = ny * nz * CORES * nx
    core = lax.rem(leaf_i, CORES)
    z = lax.rem(leaf_i // CORES, nz)
    y = leaf_i // (CORES * nz)

    def at(dy, dz, dc, dx):
        yy, zz = lax.rem(y + dy + ny, ny), lax.rem(z + dz + nz, nz)
        cc, xx = lax.rem(core + dc + CORES, CORES), lax.rem(x + dx + nx, nx)
        return ((yy * nz + zz) * CORES + cc, xx)

    def linear(d):
        return (d // nx, lax.rem(d, nx))

    steps_z = sorted(range(nz), key=lambda i: (min(i, nz - i), i))
    steps_x = sorted(range(nx), key=lambda i: (-min(i, nx - i), i))
    direct = [n for n, j in enumerate(steps_z) if min(j, nz - j) == 1]
    steps_q = sorted(
        [(i, c) for i in range(ny) for c in range(CORES)], key=lambda s: (min(s[0], ny - s[0]), s)
    )
    before = linear(lax.rem(device + devices - 1, devices))
    after = linear(lax.rem(device + 1, devices))

    loads = [
        pltpu.make_async_copy(leaf_hbm, leaf_ref, load_sem.at[2]),
        pltpu.make_async_copy(m2m_hbm, m2m_in, load_sem.at[0]),
        pltpu.make_async_copy(m2l_hbm, m2l_in, load_sem.at[1]),
    ]
    index_refs = (
        (pa_hbm, pa_ref),
        (oa_hbm, oa_ref),
        (pb_hbm, pb_ref),
        (ob_hbm, ob_ref),
        (pc_hbm, pc_ref),
        (oc_hbm, oc_ref),
        (lbs_hbm, lbs_ref),
        (lbo_hbm, lbo_ref),
        (lts_hbm, lts_ref),
        (lto_hbm, lto_ref),
    )
    indices = [
        pltpu.make_async_copy(src, dst, load_sem.at[3 + i]) for i, (src, dst) in enumerate(index_refs)
    ]
    for load in indices[0:2] + loads[0:2]:
        load.start()

    barrier = pltpu.get_barrier_semaphore()
    partners = (
        [at(0, j, 0, 0) for j in reversed(steps_z) if j]
        + [at(0, 0, 0, i) for i in steps_x if i]
        + [at(0, steps_z[n], 0, i) for n in direct for i in steps_x if i]
        + [at(j, 0, c, 0) for j, c in reversed(steps_q) if j or c]
        + [before, after]
    )
    for partner in partners:
        pl.semaphore_signal(barrier, inc=1, device_id=partner, device_id_type=MESH)
    for load in indices[2:]:
        load.start()

    def rest_of(o):
        return slice(kinds * MAIN + o * rest_pad, kinds * MAIN + o * rest_pad + rest)

    def separate(operators, whole, joined):
        for t in range(-(-k // LANES)):
            width = min(LANES, k - t * LANES)
            lanes = slice(t * LANES, t * LANES + width)
            flat[t, :, 0:width] = operators[:, :, lanes].astype(F32).reshape(k * kinds, width)
            for o in range(kinds):
                tile = flat.at[t][pl.ds(o, k, stride=kinds), :][:, 0:width].astype(BF16)
                if whole is not None:
                    whole[o, :, lanes] = tile
                first = t * LANES
                if first < MAIN:
                    joined[:, o * MAIN + first : o * MAIN + first + width] = tile
                else:
                    joined[:, rest_of(o)] = tile

    def put(o, value):
        n = value.shape[1]
        stack[o * MAIN : (o + 1) * MAIN, 0:n] = value[0:MAIN, :]
        stack[rest_of(o), 0:n] = value[MAIN:, :]

    stack[kinds * MAIN :, :] = jnp.zeros((kinds * rest_pad, stack.shape[1]), BF16)
    m2m_p[:, kinds * MAIN :] = jnp.zeros((k, kinds * rest_pad), BF16)
    m2l_p[:, kinds * MAIN :] = jnp.zeros((k, kinds * rest_pad), BF16)

    indices[0].wait()
    indices[1].wait()
    cell = (
        lax.broadcasted_iota(I32, pa_ref.shape, 0) * LANES
        + lax.broadcasted_iota(I32, pa_ref.shape, 1)
    )
    code_a = oa_ref[...] * cells_b + pa_ref[...] - device * cells_b
    code_a = jnp.where(cell < count_ref[0], code_a, -1)
    slot = lax.broadcasted_iota(I32, (8 * cells_b, LANES), 0)
    for r in range(cells_a // LANES):
        one_hot_a[:, r * LANES : (r + 1) * LANES] = (slot == code_a[r : r + 1, :]).astype(F32).astype(BF16)

    for load in loads[0:2] + indices[2:]:
        load.wait()
    loads[2].start()
    separate(m2m_in, m2m_v, m2m_p)
    for o in range(0, 8, 2):
        pair = dot(leaf_ref[...], one_hot_a[o * cells_b : (o + 2) * cells_b, :], (1, 1)).astype(BF16)
        put(o, pair[:, :cells_b])
        put(o + 1, pair[:, cells_b:])
        m2m_t[o] = m2m_v[o].T
        m2m_t[o + 1] = m2m_v[o + 1].T
    mult_b = stacked_dot(m2m_p, stack[:, :cells_b]).astype(BF16)
    window[:, cells_b : 2 * cells_b] = jnp.zeros((window.shape[0], cells_b), BF16)
    window[0:k, cells_b : 2 * cells_b] = mult_b

    code_b = ob_ref[...] * cells_c + pb_ref[...] - device * cells_c
    slots_b = 8 * cells_c
    one_hot_b = (lax.broadcasted_iota(I32, (slots_b, cells_b), 0) == code_b).astype(F32)
    grouped_c = dot(one_hot_b.astype(BF16), mult_b, (1, 1)).astype(BF16)
    mult_c = dot(grouped_c[0:cells_c, :], m2m_t[0])
    for o in range(1, 8):
        mult_c = mult_c + dot(grouped_c[o * cells_c : (o + 1) * cells_c, :], m2m_t[o])
    octant_c = column_of(oc_ref[...])
    shifted = jnp.zeros((cells_c, k), F32)
    for o in range(8):
        shifted = shifted + dot(jnp.where(octant_c == o, mult_c, 0.0).astype(BF16), m2m_t[o])
    pad_v[0:cells_c, :] = jnp.zeros((cells_c, pad_v.shape[1]), F32)
    pad_v[0:cells_c, 0:k] = shifted
    parent_c = column_of(pc_ref[...])
    high = (parent_c // 32).astype(F32)
    low = (parent_c % 32).astype(F32)
    lane = lax.broadcasted_iota(I32, (cells_c, kp), 1)
    message = jnp.where(lane == k, high, jnp.where(lane == k + 1, low, pad_v[0:cells_c, 0:kp]))
    gathered[0:cells_c, :] = message.astype(BF16)
    lane = lax.broadcasted_iota(I32, (cells_c, LANES), 1)
    heads[0:cells_c, :] = jnp.where(lane < LANES // 2, high, low).astype(BF16)

    def send(src, dst, sems, index, partner):
        copy = pltpu.make_async_remote_copy(
            src_ref=src,
            dst_ref=dst,
            send_sem=sems[0].at[index],
            recv_sem=sems[1].at[index],
            device_id=partner,
            device_id_type=MESH,
        )
        copy.start()
        return copy

    def part(ref, i):
        return ref.at[i * cells_c : (i + 1) * cells_c]

    pl.semaphore_wait(barrier, len(partners))

    sent_z, sent_x = {}, {}

    def along_x(n, source, dz):
        for i in steps_x:
            if i:
                sent_x[n, i] = send(
                    part(gathered, source), part(gathered, n * nx + i), sems_x, n * (nx - 1) + i - 1, at(0, dz, 0, i)
                )

    for n in reversed(range(1, nz)):
        sent_z[n] = send(part(gathered, 0), part(gathered, n * nx), sems_z, n - 1, at(0, steps_z[n], 0, 0))
        if n in direct:
            along_x(n, 0, steps_z[n])
    along_x(0, 0, 0)
    far_first = list(reversed(list(enumerate(steps_q))))
    sent_heads = {}
    for n, (j, c) in far_first:
        if n:
            sent_heads[n] = send(part(heads, 0), part(heads, n), sems_h, n - 1, at(j, 0, c, 0))
    def count(place, wanted, kind, store):
        weights = []
        for first in range(0, kinds, 4):
            weight = jnp.zeros(kind.shape, I32)
            for o in range(first, min(first + 4, kinds)):
                weight = jnp.where(kind == o, 1 << (8 * (o - first)), weight)
            weights.append(weight)
        sums = [jnp.zeros((place.shape[0], kind.shape[1]), I32) for _ in weights]
        for e in range(entries):
            same = place == wanted[e : e + 1, :]
            sums = [s + jnp.where(same, w[e : e + 1, :], 0) for s, w in zip(sums, weights)]
        for o in range(kinds):
            store(o, ((sums[o // 4] >> (8 * (o % 4))) & 255).astype(F32).astype(BF16))

    def store_b(o, m):
        count_b[:, o * cells_b : (o + 1) * cells_b] = m

    place_b = lax.broadcasted_iota(I32, (3 * cells_b, cells_b), 0)
    count(place_b, lbs_ref[...] - (device - 1) * cells_b, lbo_ref[...], store_b)

    loads[2].wait()
    separate(m2l_in, None, m2l_p)

    for n in range(1, nz):
        if n not in direct:
            sent_z[n].wait_recv()
            along_x(n, n * nx, 0)

    mine = window.at[:, cells_b : 2 * cells_b]
    near_sems = (near_send, near_recv)
    to_before = send(mine, window.at[:, 2 * cells_b : 3 * cells_b], near_sems, 0, before)
    to_after = send(mine, window.at[:, 0:cells_b], near_sems, 1, after)

    for n in sent_heads:
        sent_heads[n].wait_recv()
    targets = heads.shape[0]

    def parents(high, low):
        return (high.astype(F32) * 32.0 + low.astype(F32)).astype(I32)

    listed = lto_ref[...] * tops + lts_ref[...]
    split = jnp.concatenate([(listed // 128).astype(F32), (listed % 128).astype(F32)], axis=0)
    wanted = parents(heads[:, 0:1], heads[:, LANES // 2 : LANES // 2 + 1])
    wanted = (wanted == lax.broadcasted_iota(I32, (targets, tops), 1)).astype(F32)
    codes = dot(split.astype(BF16), wanted.astype(BF16), (1, 1))
    codes = (codes[0:entries, :] * 128.0 + codes[entries:, :]).astype(I32)
    source_t, kind_t = codes % tops, codes // tops

    sources = gathered.shape[0]
    half = sources // 2
    chunk = min(LANES, half)
    for first in range(0, sources, chunk):
        for n in range(first // cells_c // nx, (first + chunk) // cells_c // nx):
            if n in direct:
                sent_z[n].wait_recv()
            for i in steps_x:
                if i:
                    sent_x[n, i].wait_recv()
        here = slice(first, first + chunk)
        place = parents(gathered[here, k : k + 1], gathered[here, k + 1 : k + 2])

        def store_t(o, m):
            count_t[here, o * targets : (o + 1) * targets] = m

        count(place, source_t, kind_t, store_t)
        turned[:, here] = gathered[here, :].T
        if first + chunk == half:
            for o in range(kinds):
                lanes = slice(o * targets, (o + 1) * targets)
                early[:, lanes] = dot(turned[0:k, 0:half], count_t[0:half, lanes])

    for o in range(kinds):
        lanes = slice(o * targets, (o + 1) * targets)
        put(o, (early[:, lanes] + dot(turned[0:k, half:], count_t[half:, lanes])).astype(BF16))
    partial = stacked_dot(m2l_p, stack[:, 0:targets])
    pad_v[0:k, 0:targets] = partial
    shares[...] = pad_v[:, 0:targets].T.astype(BF16)

    sent_q = {}
    for n, (j, c) in far_first:
        if n:
            sent_q[n] = send(part(shares, n), part(arrived, n), sems_q, n - 1, at(-j, 0, -c, 0))

    to_before.wait_recv()
    to_after.wait_recv()
    for o in range(0, kinds, 2):
        pair = dot(window[0:k, :], count_b[:, o * cells_b : (o + 2) * cells_b]).astype(BF16)
        put(o, pair[:, :cells_b])
        put(o + 1, pair[:, cells_b:])
    near = stacked_dot(m2l_p, stack[:, 0:cells_b])
    pad_v[0:k, 0:cells_b] = near
    near_t[...] = pad_v[:, 0:cells_b].T
    one_hot_bt = one_hot_b.T.astype(BF16)

    top_local = shares[0:cells_c, :].astype(F32)
    for n in sent_q:
        sent_q[n].wait_recv()
    for n in sent_q:
        top_local = top_local + arrived[n * cells_c : (n + 1) * cells_c, :].astype(F32)
    top_local = top_local.astype(BF16)[:, 0:k]

    local_c = jnp.zeros((cells_c, k), F32)
    for o in range(8):
        local_c = local_c + jnp.where(octant_c == o, dot(top_local, m2m_v[o]), 0.0)
    local_c = local_c.astype(BF16)
    for o in range(8):
        prod_c[o * cells_c : (o + 1) * cells_c, :] = dot(local_c, m2m_v[o])
    full = prod_c[...]
    rounded = full.astype(BF16)
    rest = (full - rounded.astype(F32)).astype(BF16)
    far = dot(one_hot_bt, rounded) + dot(one_hot_bt, rest)
    local_b = (near_t[:, 0:k] + far).astype(BF16)
    for o in range(8):
        prod_b[o * cells_b : (o + 1) * cells_b, :] = dot(local_b, m2m_v[o]).astype(BF16)
    out_ref[...] = dot(prod_b[...], one_hot_a[...], (0, 0)).astype(BF16)

    to_before.wait_send()
    to_after.wait_send()
    for sent in (sent_z, sent_x, sent_heads, sent_q):
        for copy in sent.values():
            copy.wait_send()


def body(dims, *args):
    (
        leaf_mult,
        fine_count,
        parent_a,
        octant_a,
        parent_b,
        octant_b,
        parent_c,
        octant_c,
        list_b_src,
        list_b_off,
        list_t_src,
        list_t_off,
        m2m_ops,
        m2l_ops,
    ) = args
    ny, nz, nx = dims
    k, cells_a = leaf_mult.shape
    cells_b = parent_b.shape[0]
    cells_c = parent_c.shape[0]
    kinds = m2l_ops.shape[0]
    kp = -(-(k + 2) // LANES) * LANES
    kr = -(-k // 16) * 16
    sources = nz * nx * cells_c
    targets = ny * CORES * cells_c
    wide = max(cells_b, targets)
    stacked = kinds * (MAIN + -(-(k - MAIN) // 16) * 16)
    vmem = pl.BlockSpec(memory_space=pltpu.VMEM)
    smem = pl.BlockSpec(memory_space=pltpu.SMEM)
    hbm = pl.BlockSpec(memory_space=pl.ANY)

    def here(array):
        return pltpu.with_memory_space_constraint(array, pltpu.HBM)

    def pair(n):
        return [pltpu.SemaphoreType.DMA((n,)), pltpu.SemaphoreType.DMA((n,))]

    fine = pl.pallas_call(
        functools.partial(kernel, dims),
        out_shape=pltpu.VMEM((k, cells_a), BF16),
        in_specs=[hbm, smem] + [hbm] * 10 + [hbm, hbm],
        out_specs=vmem,
        scratch_shapes=[
            pltpu.VMEM((cells_a // LANES, LANES), I32),
            pltpu.VMEM((cells_a // LANES, LANES), I32),
            pltpu.VMEM((1, cells_b), I32),
            pltpu.VMEM((1, cells_b), I32),
            pltpu.VMEM((1, cells_c), I32),
            pltpu.VMEM((1, cells_c), I32),
            pltpu.VMEM(list_b_src.shape[::-1], I32),
            pltpu.VMEM(list_b_src.shape[::-1], I32),
            pltpu.VMEM(list_t_src.shape[::-1], I32),
            pltpu.VMEM(list_t_src.shape[::-1], I32),
            pltpu.VMEM((k, cells_a), BF16),
            pltpu.VMEM((k, 8, k), BF16),
            pltpu.VMEM((k, kinds, k), BF16),
            pltpu.VMEM((8, k, k), BF16),
            pltpu.VMEM((8, k, k), BF16),
            pltpu.VMEM((k, stacked), BF16),
            pltpu.VMEM((k, stacked), BF16),
            pltpu.VMEM((-(-k // LANES), kinds * k, LANES), F32),
            pltpu.VMEM((stacked, wide), BF16),
            pltpu.VMEM((8 * cells_b, cells_a), BF16),
            pltpu.VMEM((kr, 3 * cells_b), BF16),
            pltpu.VMEM((cells_b, kp), F32),
            pltpu.VMEM((kp, max(kp, wide)), F32),
            pltpu.VMEM((3 * cells_b, kinds * cells_b), BF16),
            pltpu.VMEM((sources, kinds * targets), BF16),
            pltpu.VMEM((sources, kp), BF16),
            pltpu.VMEM((kp, sources), BF16),
            pltpu.VMEM((k, kinds * targets), F32),
            pltpu.VMEM((targets, LANES), BF16),
            pltpu.VMEM((targets, kp), BF16),
            pltpu.VMEM((targets, kp), BF16),
            pltpu.VMEM((8 * cells_c, k), F32),
            pltpu.VMEM((8 * cells_b, k), BF16),
            pltpu.SemaphoreType.DMA((13,)),
            pltpu.SemaphoreType.DMA((2,)),
            pltpu.SemaphoreType.DMA((2,)),
            pair(nz - 1),
            pair(nz * (nx - 1)),
            pair(ny * CORES - 1),
            pair(ny * CORES - 1),
        ],
        compiler_params=pltpu.CompilerParams(
            collective_id=0, has_side_effects=True, vmem_limit_bytes=52 * 1024 * 1024
        ),
    )(
        here(leaf_mult),
        fine_count,
        here(parent_a.reshape(-1, LANES)),
        here(octant_a.reshape(-1, LANES)),
        here(parent_b.reshape(1, -1)),
        here(octant_b.reshape(1, -1)),
        here(parent_c.reshape(1, -1)),
        here(octant_c.reshape(1, -1)),
        here(list_b_src.T),
        here(list_b_off.T),
        here(list_t_src.T),
        here(list_t_off.T),
        here(m2m_ops.transpose(1, 0, 2)),
        here(m2l_ops.transpose(1, 0, 2)),
    )
    return fine


def solution(mesh):
    nx = mesh.shape["coef"]
    plane = mesh.shape["leaf"] // CORES
    nz = 1
    while nz * nz < plane:
        nz *= 2
    both = P(("leaf", "coef"))
    rows = P(("leaf", "coef"), None)
    in_specs = (P(None, ("leaf", "coef")),) + (both,) * 7 + (rows, rows) + (P(),) * 4
    return jax.shard_map(
        functools.partial(body, (plane // nz, nz, nx)),
        mesh=mesh,
        in_specs=in_specs,
        out_specs=P(None, ("leaf", "coef")),
        check_vma=False,
    )
```
